32 devices in a mesh: groups: 2 (over y), expert: 4 (over x, core), helper: 4 (over z).
Axes of the slice: x: 2, y: 2, z: 4, core: 2. Of those that a mesh axis runs over, the one named last changes fastest.
Arguments:
- activations: bfloat16 [2048, 2880], P(('groups', 'expert', 'helper')), parts along dimension 0, may hold values from -6 to 6
- expert_ids: int32 [2048, 4], P(('groups', 'expert', 'helper')), parts along dimension 0, may hold values from 0 to 7, all different within a row; in each aligned block of 64 rows (0 to 63, 64 to 127, ...) at most 64 rows name the same one
- route_gates: float32 [2048, 4], P(('groups', 'expert', 'helper')), parts along dimension 0, may hold values from 0.1 to 0.6
- inner_weight: bfloat16 [16, 2, 2880, 720], P(('expert', 'helper')), may hold values from -0.109375 to 0.109375
- outer_weight: bfloat16 [16, 720, 2880], P(('expert', 'helper')), may hold values from -0.15625 to 0.15625
Outputs:
- layer_out: bfloat16 [2048, 2880], P(('groups', 'expert', 'helper')), parts along dimension 0
The draws below stay inside these ranges and needn't reach their ends.
There are 2 independent parts, one for each index of `groups`. The reference program is written for one: setup_inputs(seed, part) draws one part's arguments, and reference() takes and returns one part's arrays. A program takes and returns all parts, laid end to end along the dimension named above; an argument that names none is the same for every part. Nothing has to cross between parts.
Inputs may be any that keep to these rules, and one draw needn't show every extreme that they name: `expert_ids`: each row names 4 different experts. Within the rows of one device (aligned blocks of 64 rows) no expert is named more than 64 times.
All inputs are finite; a program needn't handle non-finite values.
Results may differ from the reference program's by a relative error of at most 0.0066.
Values may be sent and summed in bfloat16 or wider, within the bound.
A program may use at most 128 MiB of HBM per device.

```python
import math
import jax
import jax.numpy as jnp
import numpy as np
from jax import lax

D = 2880
FF = 1440
TOPK = 4
TOK_DEV = 64
EXPERTS = 8
CAP = 64
TOKENS = 1024
N_EXPERT = 4
N_HELPER = 4


def block_levels(rng, dims, shards, smallest, high):
    level = 1.0
    for position, shards_of in shards:
        heights = jax.random.uniform(jax.random.fold_in(jax.random.fold_in(rng, 6), position), (shards_of,), jnp.float32, smallest / len(shards), high / len(shards))
        level = level * jnp.repeat(jnp.exp(heights), dims[position] // shards_of).reshape((-1,) + (1,) * (len(dims) - 1 - position))
    return level


def routed_block(rng, own, number, rows, count, top, reach, slope):
    sequence = jax.random.permutation(rng, count)
    packed, ordinary = shares(count, rows * top, reach, slope, True), shares(count, rows * top, reach, slope, False)
    places = jnp.arange(count)

    def named(sizes, rotation):
        used = int((sizes > 0).sum())
        fixed = max(1, used // 4)
        passed = fixed + (places - fixed + rotation * (used - fixed)) % max(1, count - fixed)
        return jnp.zeros((count,), jnp.int32).at[sequence[jnp.where(places < fixed, places, passed)]].set(jnp.asarray(sizes, jnp.int32))

    sizes = jnp.where(number % 4 == 0, named(packed, number // 4), named(ordinary, number - number // 4 - 1))
    mixed = jax.random.permutation(jax.random.fold_in(own, 3), count)
    source_of, taker = mixed[0:count // 2 * 2:2], mixed[1:count // 2 * 2:2]
    room = jnp.minimum(sizes[source_of] - 1, reach - sizes[taker]) // 2
    room = jnp.where((source_of == sequence[0]) | (taker == sequence[0]) | (sizes[taker] == 0), 0, jnp.maximum(room, 0))
    passed = jax.random.randint(jax.random.fold_in(own, 4), (count // 2,), 0, 1 << 20) % (room + 1)
    sizes = sizes.at[source_of].add(-passed).at[taker].add(passed)
    members = jnp.searchsorted(jnp.cumsum(sizes), jnp.arange(rows * top), side="right").astype(jnp.int32)
    grid = members.reshape(top, rows).T
    grid = grid[jax.random.permutation(jax.random.fold_in(own, 1), rows)]
    rotation = jax.random.randint(jax.random.fold_in(own, 2), (rows, 1), 0, top)
    return jnp.take_along_axis(grid, (jnp.arange(top)[None, :] + rotation) % top, axis=1)


def shares(amount, total, most, slope, full):
    loads = [(1 << 20) // math.isqrt(grade ** slope) + 1 for grade in range(1, amount + 1)]
    largest = most if full else min(most, max(-(-total // amount), total * loads[0] // sum(loads)))
    least = 1 if total - largest >= amount - 1 else 0
    counts, rest = [largest] + [least] * (amount - 1), total - largest - least * (amount - 1)
    while rest > 0:
        free = [i for i in range(1, amount) if counts[i] < largest] or [i for i in range(1, amount) if counts[i] < most]
        pool, budget = sum([loads[i] for i in free]), rest
        for i in free:
            extra = min(most - counts[i], max(1, budget * loads[i] // pool), rest)
            counts[i] = counts[i] + extra
            rest = rest - extra
    return np.array(counts)


def noise(rng, extent, width, limit, shards=(), kind=jnp.bfloat16):
    array = jax.random.normal(rng, extent, jnp.float32) * width
    if len(shards) > 0:
        array = block_levels(rng, extent, shards, -0.22, 0.18) * array
    return jnp.clip(array, min=-limit, max=limit).astype(kind)


def setup_inputs(seed: int = 0, part: int = 0) -> dict:
    arg_keys = jax.random.split(jax.random.key(seed), 6)
    own_keys = jax.random.split(jax.random.fold_in(arg_keys[5], part), 6)
    activations = noise(own_keys[0], (TOKENS, D), 1.0, 6.0, ((0, 16),))
    expert_ids_keys = jax.random.split(jax.random.fold_in(own_keys[1], 1), TOKENS // TOK_DEV)
    expert_ids_turns = jax.random.permutation(jax.random.fold_in(own_keys[1], 3), TOKENS // TOK_DEV)
    expert_ids = jax.vmap(lambda own, number: routed_block(jax.random.fold_in(own_keys[1], 2), own, number, TOK_DEV, EXPERTS, TOPK, CAP, 2))(expert_ids_keys, expert_ids_turns).reshape((TOKENS, TOPK))
    route_gates = jnp.clip(0.1 + 0.5 * jax.random.uniform(own_keys[2], (TOKENS, TOPK), jnp.float32) ** block_levels(own_keys[2], (TOKENS, TOPK), ((0, 16),), -0.2, 0.2), 0.1, 0.6)
    inner_weight = noise(arg_keys[3], (2 * EXPERTS, 2, D, FF // 2), D ** -0.5, 0.109375, ((0, 16),))
    outer_weight = noise(arg_keys[4], (2 * EXPERTS, FF // 2, D), FF ** -0.5, 0.15625, ((0, 16),))
    return {"activations": activations, "expert_ids": expert_ids, "route_gates": route_gates, "inner_weight": inner_weight, "outer_weight": outer_weight}


def reference(activations, expert_ids, route_gates, inner_weight, outer_weight):
    devices_all = N_EXPERT * N_HELPER
    assigned = TOK_DEV * TOPK
    flat_ids = expert_ids.reshape(devices_all, assigned)
    onehot = (flat_ids[:, :, None] == jnp.arange(EXPERTS, dtype=jnp.int32)[None, None, :]).astype(jnp.int32)
    ranking = jnp.sum(jnp.cumsum(onehot, axis=1) * onehot, axis=2) - 1
    source = jnp.arange(devices_all, dtype=jnp.int32)[:, None]
    slot_index = ((flat_ids * devices_all + source) * CAP + ranking).reshape(-1).astype(jnp.int32)
    token_index = (jnp.arange(TOKENS * TOPK, dtype=jnp.int32) // TOPK).astype(jnp.int32)
    buffer = jnp.zeros((EXPERTS * devices_all * CAP, D), jnp.bfloat16)
    buffer = buffer.at[slot_index].set(activations[token_index])
    blocks = buffer.reshape(EXPERTS, devices_all * CAP, D)
    inner_split = inner_weight.reshape(EXPERTS, 2, 2, D, FF // 2)
    outer_split = outer_weight.reshape(EXPERTS, 2, FF // 2, D)

    def expert_step(operands):
        slot_rows, weights_in, weights_out = operands
        gate_proj = jnp.concatenate([
            jnp.dot(slot_rows, weights_in[0, 0], preferred_element_type=jnp.float32),
            jnp.dot(slot_rows, weights_in[1, 0], preferred_element_type=jnp.float32)], axis=1)
        up_proj = jnp.concatenate([
            jnp.dot(slot_rows, weights_in[0, 1], preferred_element_type=jnp.float32),
            jnp.dot(slot_rows, weights_in[1, 1], preferred_element_type=jnp.float32)], axis=1)
        hidden = ((up_proj + 1.0) * gate_proj * jax.nn.sigmoid(1.702 * gate_proj)).astype(jnp.bfloat16)
        half_width = FF // 2
        first_out = jnp.dot(hidden[:, :half_width], weights_out[0], preferred_element_type=jnp.float32).astype(jnp.bfloat16)
        second_out = jnp.dot(hidden[:, half_width:], weights_out[1], preferred_element_type=jnp.float32).astype(jnp.bfloat16)
        first_out = lax.optimization_barrier(first_out)
        second_out = lax.optimization_barrier(second_out)
        return (first_out.astype(jnp.float32) + second_out.astype(jnp.float32)).astype(jnp.bfloat16)

    results = lax.map(expert_step, (blocks, inner_split, outer_split))
    picked = results.reshape(-1, D)[slot_index].astype(jnp.float32).reshape(TOKENS, TOPK, D)
    combined = jnp.sum(picked * route_gates[:, :, None], axis=1)
    return combined.astype(jnp.bfloat16)
```

```python
import jax
import jax.numpy as jnp
from jax import lax
from jax.sharding import PartitionSpec as P


def swapped(shard, axis, bit):
    return lax.ppermute(shard, axis, [(i, i ^ 1 << bit) for i in range(lax.axis_size(axis))])


def deliver(outgoing):
    return lax.all_to_all(outgoing, ("expert", "helper"), split_axis=0, concat_axis=0, tiled=True)


def send_back(outgoing):
    return lax.all_to_all(outgoing, ("expert", "helper"), split_axis=0, concat_axis=0, tiled=True)


def routed_body(activations, expert_ids, route_gates, inner_weight, outer_weight):
    tok_count, model_width = activations.shape
    top_count = expert_ids.shape[1]
    devices_all = lax.axis_size("expert") * lax.axis_size("helper")
    experts_all = devices_all // 2
    capacity = 2 * max(1, tok_count * top_count // experts_all)
    half_cap = capacity // 2
    flat_ids = expert_ids.reshape(-1)
    onehot = (flat_ids[:, None] == jnp.arange(experts_all, dtype=jnp.int32)[None, :]).astype(
        jnp.int32
    )
    ranking = jnp.sum(jnp.cumsum(onehot, axis=0) * onehot, axis=1) - 1
    slot_index = flat_ids * capacity + ranking
    token_index = jnp.arange(flat_ids.shape[0], dtype=jnp.int32) // top_count
    buffer = jnp.zeros((experts_all * capacity, model_width), activations.dtype)
    buffer = buffer.at[slot_index].set(activations[token_index])
    parity = lax.axis_index("helper") % 2
    arrived = deliver(jnp.repeat(buffer.reshape(experts_all, capacity, model_width), 2, axis=0))
    slot_rows = arrived.reshape(-1, model_width)
    projected = jnp.einsum(
        "rd,cdf->crf", slot_rows, inner_weight[0], preferred_element_type=jnp.float32
    )
    gate_proj = projected[0]
    up_proj = projected[1]
    hidden = ((up_proj + 1.0) * gate_proj * jax.nn.sigmoid(1.702 * gate_proj)).astype(jnp.bfloat16)
    partial_value = jnp.dot(hidden, outer_weight[0], preferred_element_type=jnp.float32).astype(
        jnp.bfloat16
    )
    partial_value = partial_value.reshape(devices_all, capacity, model_width)
    first_part = partial_value[:, :half_cap]
    second_part = partial_value[:, half_cap:]
    kept_half = jnp.where(parity == 0, first_part, second_part)
    given_half = jnp.where(parity == 0, second_part, first_part)
    received_half = swapped(given_half, "helper", 0)
    kept_half = lax.optimization_barrier(kept_half)
    summed = kept_half.astype(jnp.float32) + received_half.astype(jnp.float32)
    results = summed.astype(jnp.bfloat16)
    returned = send_back(results).reshape(experts_all * capacity, model_width)
    picked = returned[slot_index].astype(jnp.float32).reshape(tok_count, top_count, model_width)
    combined = jnp.sum(picked * route_gates[:, :, None], axis=1)
    return combined.astype(jnp.bfloat16)


AXES = ("expert", "helper")


def dense_body(activations, expert_ids, route_gates, inner_weight, outer_weight):
    experts_all = lax.axis_size("expert") * lax.axis_size("helper") // 2
    expert = (lax.axis_index("expert") * lax.axis_size("helper") + lax.axis_index("helper")) // 2
    named = expert_ids[:, :, None] == jnp.arange(experts_all, dtype=jnp.int32)[None, None, :]
    weights = jnp.sum(jnp.where(named, route_gates[:, :, None], 0.0), axis=1)
    rows = lax.all_gather(activations, AXES, axis=0, tiled=True)
    weights = lax.all_gather(weights, AXES, axis=0, tiled=True)
    own = jnp.sum(jnp.where(jnp.arange(experts_all)[None, :] == expert, weights, 0.0), axis=1)
    gate_proj = jnp.dot(rows, inner_weight[0, 0], preferred_element_type=jnp.float32)
    up_proj = jnp.dot(rows, inner_weight[0, 1], preferred_element_type=jnp.float32)
    hidden = ((up_proj + 1.0) * gate_proj * jax.nn.sigmoid(1.702 * gate_proj)).astype(jnp.bfloat16)
    partial = jnp.dot(hidden, outer_weight[0], preferred_element_type=jnp.float32)
    partial = (partial * own[:, None]).astype(jnp.bfloat16)
    return lax.psum_scatter(partial, AXES, scatter_dimension=0, tiled=True)


def body(activations, expert_ids, route_gates, inner_weight, outer_weight):
    tok_count, top_count = expert_ids.shape
    experts_all = lax.axis_size("expert") * lax.axis_size("helper") // 2
    capacity = 2 * max(1, tok_count * top_count // experts_all)
    chosen = dense_body if capacity >= tok_count else routed_body
    return chosen(activations, expert_ids, route_gates, inner_weight, outer_weight)


def solution(mesh):
    placed = (
        P(("groups", "expert", "helper"), None),
        P(("groups", "expert", "helper"), None),
        P(("groups", "expert", "helper"), None),
        P(("expert", "helper"), None, None, None),
        P(("expert", "helper"), None, None),
    )
    return jax.shard_map(
        body,
        mesh=mesh,
        in_specs=placed,
        out_specs=P(("groups", "expert", "helper"), None),
        check_vma=False,
    )
```

```python
import jax
import jax.numpy as jnp
from jax import lax
from jax.experimental import pallas as pl
from jax.experimental.pallas import tpu as pltpu
from jax.sharding import PartitionSpec as P


def swapped(shard, axis, bit):
    return lax.ppermute(shard, axis, [(i, i ^ 1 << bit) for i in range(lax.axis_size(axis))])


def deliver(outgoing):
    return lax.all_to_all(outgoing, ("expert", "helper"), split_axis=0, concat_axis=0, tiled=True)


def send_back(outgoing):
    return lax.all_to_all(outgoing, ("expert", "helper"), split_axis=0, concat_axis=0, tiled=True)


def routed_body(activations, expert_ids, route_gates, inner_weight, outer_weight):
    tok_count, model_width = activations.shape
    top_count = expert_ids.shape[1]
    devices_all = lax.axis_size("expert") * lax.axis_size("helper")
    experts_all = devices_all // 2
    capacity = 2 * max(1, tok_count * top_count // experts_all)
    half_cap = capacity // 2
    flat_ids = expert_ids.reshape(-1)
    onehot = (flat_ids[:, None] == jnp.arange(experts_all, dtype=jnp.int32)[None, :]).astype(
        jnp.int32
    )
    ranking = jnp.sum(jnp.cumsum(onehot, axis=0) * onehot, axis=1) - 1
    slot_index = flat_ids * capacity + ranking
    token_index = jnp.arange(flat_ids.shape[0], dtype=jnp.int32) // top_count
    buffer = jnp.zeros((experts_all * capacity, model_width), activations.dtype)
    buffer = buffer.at[slot_index].set(activations[token_index])
    parity = lax.axis_index("helper") % 2
    arrived = deliver(jnp.repeat(buffer.reshape(experts_all, capacity, model_width), 2, axis=0))
    slot_rows = arrived.reshape(-1, model_width)
    projected = jnp.einsum(
        "rd,cdf->crf", slot_rows, inner_weight[0], preferred_element_type=jnp.float32
    )
    gate_proj = projected[0]
    up_proj = projected[1]
    hidden = ((up_proj + 1.0) * gate_proj * jax.nn.sigmoid(1.702 * gate_proj)).astype(jnp.bfloat16)
    partial_value = jnp.dot(hidden, outer_weight[0], preferred_element_type=jnp.float32).astype(
        jnp.bfloat16
    )
    partial_value = partial_value.reshape(devices_all, capacity, model_width)
    first_part = partial_value[:, :half_cap]
    second_part = partial_value[:, half_cap:]
    kept_half = jnp.where(parity == 0, first_part, second_part)
    given_half = jnp.where(parity == 0, second_part, first_part)
    received_half = swapped(given_half, "helper", 0)
    kept_half = lax.optimization_barrier(kept_half)
    summed = kept_half.astype(jnp.float32) + received_half.astype(jnp.float32)
    results = summed.astype(jnp.bfloat16)
    returned = send_back(results).reshape(experts_all * capacity, model_width)
    picked = returned[slot_index].astype(jnp.float32).reshape(tok_count, top_count, model_width)
    combined = jnp.sum(picked * route_gates[:, :, None], axis=1)
    return combined.astype(jnp.bfloat16)


AXES = ("expert", "helper")


def dense_body(activations, expert_ids, route_gates, inner_weight, outer_weight):
    experts_all = lax.axis_size("expert") * lax.axis_size("helper") // 2
    expert = (lax.axis_index("expert") * lax.axis_size("helper") + lax.axis_index("helper")) // 2
    named = expert_ids[:, :, None] == jnp.arange(experts_all, dtype=jnp.int32)[None, None, :]
    weights = jnp.sum(jnp.where(named, route_gates[:, :, None], 0.0), axis=1)
    rows = lax.all_gather(activations, AXES, axis=0, tiled=True)
    weights = lax.all_gather(weights, AXES, axis=0, tiled=True)
    own = jnp.sum(jnp.where(jnp.arange(experts_all)[None, :] == expert, weights, 0.0), axis=1)
    gate_proj = jnp.dot(rows, inner_weight[0, 0], preferred_element_type=jnp.float32)
    up_proj = jnp.dot(rows, inner_weight[0, 1], preferred_element_type=jnp.float32)
    hidden = ((up_proj + 1.0) * gate_proj * jax.nn.sigmoid(1.702 * gate_proj)).astype(jnp.bfloat16)
    partial = jnp.dot(hidden, outer_weight[0], preferred_element_type=jnp.float32)
    partial = (partial * own[:, None]).astype(jnp.bfloat16)
    return lax.psum_scatter(partial, AXES, scatter_dimension=0, tiled=True)


UP, DOWN, ACROSS, TWIN = 0, 1, 2, 3


def line_kernel(
    rows_ref, inner_ref, outer_ref, out_ref,
    rows, inner, outer, parts, twin_in, cross_out, cross_in, line_out, line_up, line_down,
    gather_send, gather_recv, twin_send, twin_recv, cross_send, cross_recv,
    up_send, up_recv, down_send, down_recv, weight_sem,
):
    length = 4
    tok, width = out_ref.shape
    me = lax.axis_index("expert")
    z = lax.axis_index("helper")
    x, core = me // 2, me % 2
    spare = rows_ref.shape[1] - 128
    experts_all = lax.axis_size("expert") * lax.axis_size("helper") // 2
    expert = (me * length + z) // 2
    up_dev = {"helper": jnp.minimum(z + 1, length - 1)}
    down_dev = {"helper": jnp.maximum(z - 1, 0)}
    cross_dev = {"expert": (1 - x) * 2 + core}
    twin_dev = {"expert": x * 2 + (1 - core)}
    devs = (up_dev, down_dev, cross_dev, twin_dev)
    has_up, has_down = z < length - 1, z > 0
    own_slot = core * 2 + x
    cross_slot = core * 2 + (1 - x)

    load_inner = pltpu.make_async_copy(inner_ref, inner, weight_sem.at[0])
    load_outer = pltpu.make_async_copy(outer_ref, outer, weight_sem.at[1])
    load_inner.start()
    load_outer.start()

    barrier = pltpu.get_barrier_semaphore()

    def greet(dev):
        pl.semaphore_signal(barrier, inc=1, device_id=dev, device_id_type=pl.DeviceIdType.MESH)

    greet(cross_dev)
    greet(twin_dev)

    @pl.when(has_up)
    def _():
        greet(up_dev)

    @pl.when(has_down)
    def _():
        greet(down_dev)

    rows[z, own_slot] = rows_ref[...]
    pl.semaphore_wait(barrier, jnp.where(has_up & has_down, 4, 3))

    def block_copy(way, plane, slot):
        return pltpu.make_async_remote_copy(
            src_ref=rows.at[plane, slot], dst_ref=rows.at[plane, slot],
            send_sem=gather_send.at[way, plane, slot], recv_sem=gather_recv.at[plane, slot],
            device_id=devs[way], device_id_type=pl.DeviceIdType.MESH,
        )

    def moved(src, dst, send, recv, dev, at):
        return pltpu.make_async_remote_copy(
            src_ref=src, dst_ref=dst.at[at], send_sem=send.at[at], recv_sem=recv.at[at],
            device_id=dev, device_id_type=pl.DeviceIdType.MESH,
        )

    def twin_copy(plane):
        return moved(parts.at[plane, pl.ds((1 - core) * 2, 2)], twin_in, twin_send, twin_recv, twin_dev, plane)

    def cross_copy(plane):
        return moved(cross_out.at[plane], cross_in, cross_send, cross_recv, cross_dev, plane)

    def up_copy(plane):
        return moved(line_out.at[plane], line_up, up_send, up_recv, up_dev, plane)

    def down_copy(plane):
        return moved(line_out.at[plane], line_down, down_send, down_recv, down_dev, plane)

    def plane_of(i):
        second = jnp.where(z == 0, 1, z - 1)
        third = jnp.where(z == 0, 2, jnp.where(z == 3, 1, z + 1))
        fourth = jnp.where(z <= 1, 3, 0)
        return jnp.where(i == 0, z, jnp.where(i == 1, second, jnp.where(i == 2, third, fourth)))

    @pl.when(has_up)
    def _():
        block_copy(UP, z, own_slot).start()

    @pl.when(has_down)
    def _():
        block_copy(DOWN, z, own_slot).start()

    block_copy(ACROSS, z, own_slot).start()
    block_copy(TWIN, z, own_slot).start()

    def shift_in(dist):
        @pl.when(z - dist >= 0)
        def _():
            plane = jnp.maximum(z - dist, 0)
            block_copy(UP, plane, own_slot).wait_recv()

            @pl.when(has_up)
            def _():
                block_copy(UP, plane, own_slot).start()

            block_copy(ACROSS, plane, own_slot).start()
            block_copy(TWIN, plane, own_slot).start()

        @pl.when(z + dist <= length - 1)
        def _():
            plane = jnp.minimum(z + dist, length - 1)
            block_copy(DOWN, plane, own_slot).wait_recv()

            @pl.when(has_down)
            def _():
                block_copy(DOWN, plane, own_slot).start()

            block_copy(ACROSS, plane, own_slot).start()
            block_copy(TWIN, plane, own_slot).start()

    def expert_part(plane):
        group = rows[plane].reshape(4 * tok, rows_ref.shape[1])
        lane = lax.broadcasted_iota(jnp.int32, (4 * tok, 128), 1)
        first = width - spare + expert
        mine = (lane == first) | (lane == first + experts_all) | (lane == first + 2 * experts_all)
        tail = rows[plane, :, :, pl.ds(spare, 128)].reshape(4 * tok, 128).astype(jnp.float32)
        gain = jnp.sum(jnp.where(mine, tail, 0.0), axis=1, keepdims=True)
        group = group[:, :width]
        over = (((1,), (1,)), ((), ()))
        gate_proj = lax.dot_general(group, inner[0], over, preferred_element_type=jnp.float32)
        up_proj = lax.dot_general(group, inner[1], over, preferred_element_type=jnp.float32)
        hidden = ((up_proj + 1.0) * gate_proj * jax.nn.sigmoid(1.702 * gate_proj)).astype(jnp.bfloat16)
        for low in range(0, width, 1024):
            high = min(low + 1024, width)
            value = jnp.dot(hidden, outer[:, low:high], preferred_element_type=jnp.float32) * gain
            parts[plane, :, :, low:high] = value.astype(jnp.bfloat16).reshape(4, tok, high - low)

    def cross_sum(plane):
        twin_copy(plane).wait_recv()
        total = parts[plane, cross_slot].astype(jnp.float32) + twin_in[plane, 1 - x].astype(jnp.float32)
        cross_out[plane] = total.astype(jnp.bfloat16)
        cross_copy(plane).start()

    def step(i, carry):
        plane = plane_of(i)

        @pl.when(i < length - 1)
        def _():
            shift_in(i + 1)

        block_copy(ACROSS, plane, cross_slot).wait_recv()
        block_copy(TWIN, plane, cross_slot).start()
        for other in range(2):
            block_copy(TWIN, plane, (1 - core) * 2 + other).wait_recv()

        @pl.when(i == 0)
        def _():
            load_inner.wait()
            load_outer.wait()

        expert_part(plane)
        twin_copy(plane).start()

        @pl.when(i >= 1)
        def _():
            cross_sum(plane_of(i - 1))

        return carry

    lax.fori_loop(0, length, step, 0)
    cross_sum(plane_of(3))

    def column_sum(plane):
        cross_copy(plane).wait_recv()
        return (
            parts[plane, own_slot].astype(jnp.float32)
            + twin_in[plane, x].astype(jnp.float32)
            + cross_in[plane].astype(jnp.float32)
        )

    def line_step(j, carry):
        first = jnp.where(z <= 1, z + 1, z - 1)
        second = jnp.where(z <= 1, z + 2, z - 2)
        third = jnp.where(z == 0, 3, jnp.where(z == 1, 0, jnp.where(z == 2, 3, 0)))
        plane = jnp.where(j == 0, first, jnp.where(j == 1, second, third))
        total = column_sum(plane)

        @pl.when(plane > z)
        def _():
            @pl.when(has_down)
            def _():
                up_copy(plane).wait_recv()
                line_out[plane] = (total + line_up[plane].astype(jnp.float32)).astype(jnp.bfloat16)

            @pl.when(z == 0)
            def _():
                line_out[plane] = total.astype(jnp.bfloat16)

            up_copy(plane).start()

        @pl.when(plane < z)
        def _():
            @pl.when(has_up)
            def _():
                down_copy(plane).wait_recv()
                line_out[plane] = (total + line_down[plane].astype(jnp.float32)).astype(jnp.bfloat16)

            @pl.when(z == length - 1)
            def _():
                line_out[plane] = total.astype(jnp.bfloat16)

            down_copy(plane).start()

        return carry

    lax.fori_loop(0, length - 1, line_step, 0)
    total = column_sum(z)

    @pl.when(z == 0)
    def _():
        down_copy(z).wait_recv()
        out_ref[...] = (total + line_down[z].astype(jnp.float32)).astype(jnp.bfloat16)

    @pl.when(z == length - 1)
    def _():
        up_copy(z).wait_recv()
        out_ref[...] = (total + line_up[z].astype(jnp.float32)).astype(jnp.bfloat16)

    @pl.when(has_up & has_down)
    def _():
        up_copy(z).wait_recv()
        down_copy(z).wait_recv()
        both = line_up[z].astype(jnp.float32) + line_down[z].astype(jnp.float32)
        out_ref[...] = (total + both).astype(jnp.bfloat16)

    def drain(plane, carry):
        @pl.when(has_up & (plane <= z))
        def _():
            block_copy(UP, plane, own_slot).wait_send()

        @pl.when(has_down & (plane >= z))
        def _():
            block_copy(DOWN, plane, own_slot).wait_send()

        block_copy(ACROSS, plane, own_slot).wait_send()
        block_copy(TWIN, plane, own_slot).wait_send()
        block_copy(TWIN, plane, cross_slot).wait_send()
        twin_copy(plane).wait_send()
        cross_copy(plane).wait_send()

        @pl.when(plane > z)
        def _():
            up_copy(plane).wait_send()

        @pl.when(plane < z)
        def _():
            down_copy(plane).wait_send()

        return carry

    lax.fori_loop(0, length, drain, 0)


def line_body(activations, expert_ids, route_gates, inner_weight, outer_weight):
    tok, width = activations.shape
    hidden = outer_weight.shape[1]
    length = lax.axis_size("helper")
    experts_all = lax.axis_size("expert") * length // 2
    named = expert_ids[:, :, None] == jnp.arange(experts_all, dtype=jnp.int32)[None, None, :]
    weights = jnp.sum(jnp.where(named, route_gates[:, :, None], 0.0), axis=1)
    high = lax.reduce_precision(weights, 8, 7)
    middle = lax.reduce_precision(weights - high, 8, 7)
    low = weights - high - middle
    gates = jnp.concatenate([high, middle, low], axis=1).astype(jnp.bfloat16)
    whole = -(-width // 128) * 128
    rows = jnp.concatenate([activations, jnp.pad(gates, ((0, 0), (0, whole - width - gates.shape[1])))], axis=1)
    inner = jnp.swapaxes(inner_weight[0], 1, 2)
    bf16 = jnp.bfloat16
    dma = pltpu.SemaphoreType.DMA
    block = pltpu.VMEM((length, tok, width), bf16)
    return pl.pallas_call(
        line_kernel,
        out_shape=jax.ShapeDtypeStruct((tok, width), bf16),
        in_specs=[
            pl.BlockSpec(memory_space=pltpu.VMEM),
            pl.BlockSpec(memory_space=pl.ANY),
            pl.BlockSpec(memory_space=pl.ANY),
        ],
        out_specs=pl.BlockSpec(memory_space=pltpu.VMEM),
        scratch_shapes=[
            pltpu.VMEM((length, 4, tok, whole), bf16),
            pltpu.VMEM((2, hidden, width), bf16),
            pltpu.VMEM((hidden, width), bf16),
            pltpu.VMEM((length, 4, tok, width), bf16),
            pltpu.VMEM((length, 2, tok, width), bf16),
            block, block, block, block, block,
            dma((4, length, 4)), dma((length, 4)),
            dma((length,)), dma((length,)), dma((length,)), dma((length,)),
            dma((length,)), dma((length,)), dma((length,)), dma((length,)),
            dma((2,)),
        ],
        compiler_params=pltpu.CompilerParams(
            collective_id=0, has_side_effects=True, vmem_limit_bytes=58 * 1024 * 1024
        ),
    )(rows, inner, outer_weight[0])


def body(activations, expert_ids, route_gates, inner_weight, outer_weight):
    tok_count, top_count = expert_ids.shape
    experts_all = lax.axis_size("expert") * lax.axis_size("helper") // 2
    capacity = 2 * max(1, tok_count * top_count // experts_all)
    spare = -activations.shape[1] % 128
    four = lax.axis_size("expert") == 4 and lax.axis_size("helper") == 4
    if capacity < tok_count:
        chosen = routed_body
    elif four and tok_count % 16 == 0 and spare >= 3 * experts_all:
        chosen = line_body
    else:
        chosen = dense_body
    return chosen(activations, expert_ids, route_gates, inner_weight, outer_weight)


def solution(mesh):
    placed = (
        P(("groups", "expert", "helper"), None),
        P(("groups", "expert", "helper"), None),
        P(("groups", "expert", "helper"), None),
        P(("expert", "helper"), None, None, None),
        P(("expert", "helper"), None, None),
    )
    return jax.shard_map(
        body,
        mesh=mesh,
        in_specs=placed,
        out_specs=P(("groups", "expert", "helper"), None),
        check_vma=False,
    )
```

```python
import jax
import jax.numpy as jnp
from jax import lax
from jax.experimental import pallas as pl
from jax.experimental.pallas import tpu as pltpu
from jax.sharding import PartitionSpec as P


def swapped(shard, axis, bit):
    return lax.ppermute(shard, axis, [(i, i ^ 1 << bit) for i in range(lax.axis_size(axis))])


def deliver(outgoing):
    return lax.all_to_all(outgoing, ("expert", "helper"), split_axis=0, concat_axis=0, tiled=True)


def send_back(outgoing):
    return lax.all_to_all(outgoing, ("expert", "helper"), split_axis=0, concat_axis=0, tiled=True)


def routed_body(activations, expert_ids, route_gates, inner_weight, outer_weight):
    tok_count, model_width = activations.shape
    top_count = expert_ids.shape[1]
    devices_all = lax.axis_size("expert") * lax.axis_size("helper")
    experts_all = devices_all // 2
    capacity = 2 * max(1, tok_count * top_count // experts_all)
    half_cap = capacity // 2
    flat_ids = expert_ids.reshape(-1)
    onehot = (flat_ids[:, None] == jnp.arange(experts_all, dtype=jnp.int32)[None, :]).astype(
        jnp.int32
    )
    ranking = jnp.sum(jnp.cumsum(onehot, axis=0) * onehot, axis=1) - 1
    slot_index = flat_ids * capacity + ranking
    token_index = jnp.arange(flat_ids.shape[0], dtype=jnp.int32) // top_count
    buffer = jnp.zeros((experts_all * capacity, model_width), activations.dtype)
    buffer = buffer.at[slot_index].set(activations[token_index])
    parity = lax.axis_index("helper") % 2
    arrived = deliver(jnp.repeat(buffer.reshape(experts_all, capacity, model_width), 2, axis=0))
    slot_rows = arrived.reshape(-1, model_width)
    projected = jnp.einsum(
        "rd,cdf->crf", slot_rows, inner_weight[0], preferred_element_type=jnp.float32
    )
    gate_proj = projected[0]
    up_proj = projected[1]
    hidden = ((up_proj + 1.0) * gate_proj * jax.nn.sigmoid(1.702 * gate_proj)).astype(jnp.bfloat16)
    partial_value = jnp.dot(hidden, outer_weight[0], preferred_element_type=jnp.float32).astype(
        jnp.bfloat16
    )
    partial_value = partial_value.reshape(devices_all, capacity, model_width)
    first_part = partial_value[:, :half_cap]
    second_part = partial_value[:, half_cap:]
    kept_half = jnp.where(parity == 0, first_part, second_part)
    given_half = jnp.where(parity == 0, second_part, first_part)
    received_half = swapped(given_half, "helper", 0)
    kept_half = lax.optimization_barrier(kept_half)
    summed = kept_half.astype(jnp.float32) + received_half.astype(jnp.float32)
    results = summed.astype(jnp.bfloat16)
    returned = send_back(results).reshape(experts_all * capacity, model_width)
    picked = returned[slot_index].astype(jnp.float32).reshape(tok_count, top_count, model_width)
    combined = jnp.sum(picked * route_gates[:, :, None], axis=1)
    return combined.astype(jnp.bfloat16)


AXES = ("expert", "helper")


def dense_body(activations, expert_ids, route_gates, inner_weight, outer_weight):
    experts_all = lax.axis_size("expert") * lax.axis_size("helper") // 2
    expert = (lax.axis_index("expert") * lax.axis_size("helper") + lax.axis_index("helper")) // 2
    named = expert_ids[:, :, None] == jnp.arange(experts_all, dtype=jnp.int32)[None, None, :]
    weights = jnp.sum(jnp.where(named, route_gates[:, :, None], 0.0), axis=1)
    rows = lax.all_gather(activations, AXES, axis=0, tiled=True)
    weights = lax.all_gather(weights, AXES, axis=0, tiled=True)
    own = jnp.sum(jnp.where(jnp.arange(experts_all)[None, :] == expert, weights, 0.0), axis=1)
    gate_proj = jnp.dot(rows, inner_weight[0, 0], preferred_element_type=jnp.float32)
    up_proj = jnp.dot(rows, inner_weight[0, 1], preferred_element_type=jnp.float32)
    hidden = ((up_proj + 1.0) * gate_proj * jax.nn.sigmoid(1.702 * gate_proj)).astype(jnp.bfloat16)
    partial = jnp.dot(hidden, outer_weight[0], preferred_element_type=jnp.float32)
    partial = (partial * own[:, None]).astype(jnp.bfloat16)
    return lax.psum_scatter(partial, AXES, scatter_dimension=0, tiled=True)


UP, DOWN, ACROSS, TWIN = 0, 1, 2, 3


def line_kernel(
    rows_ref, inner_ref, outer_ref, out_ref,
    rows, inner, outer, parts, twin_in, cross_out, cross_in, line_out, line_up, line_down,
    gather_send, gather_recv, twin_send, twin_recv, cross_send, cross_recv, late_out, late_in, late_sem,
    up_send, up_recv, down_send, down_recv, weight_sem,
):
    length = 4
    tok, width = out_ref.shape
    me = lax.axis_index("expert")
    z = lax.axis_index("helper")
    x, core = me // 2, me % 2
    spare = rows_ref.shape[1] - 128
    experts_all = lax.axis_size("expert") * lax.axis_size("helper") // 2
    expert = (me * length + z) // 2
    up_dev = {"helper": jnp.minimum(z + 1, length - 1)}
    down_dev = {"helper": jnp.maximum(z - 1, 0)}
    cross_dev = {"expert": (1 - x) * 2 + core}
    twin_dev = {"expert": x * 2 + (1 - core)}
    devs = (up_dev, down_dev, cross_dev, twin_dev)
    has_up, has_down = z < length - 1, z > 0
    at_end = (z == 0) | (z == length - 1)
    half = tok // 2
    own_slot = core * 2 + x
    cross_slot = core * 2 + (1 - x)

    load_inner = pltpu.make_async_copy(inner_ref, inner, weight_sem.at[0])
    load_outer = pltpu.make_async_copy(outer_ref, outer, weight_sem.at[1])
    load_inner.start()
    load_outer.start()

    barrier = pltpu.get_barrier_semaphore()

    def greet(dev):
        pl.semaphore_signal(barrier, inc=1, device_id=dev, device_id_type=pl.DeviceIdType.MESH)

    greet(cross_dev)
    greet(twin_dev)

    @pl.when(has_up)
    def _():
        greet(up_dev)

    @pl.when(has_down)
    def _():
        greet(down_dev)

    rows[z, own_slot] = rows_ref[...]
    pl.semaphore_wait(barrier, jnp.where(has_up & has_down, 4, 3))

    def block_copy(way, plane, slot):
        return pltpu.make_async_remote_copy(
            src_ref=rows.at[plane, slot], dst_ref=rows.at[plane, slot],
            send_sem=gather_send.at[way, plane, slot], recv_sem=gather_recv.at[plane, slot],
            device_id=devs[way], device_id_type=pl.DeviceIdType.MESH,
        )

    def sem_at(ref, at):
        return ref.at[at[0], at[1]] if isinstance(at, tuple) else ref.at[at]

    def moved(src, dst, send, recv, dev, at):
        return pltpu.make_async_remote_copy(
            src_ref=src, dst_ref=sem_at(dst, at), send_sem=sem_at(send, at), recv_sem=sem_at(recv, at),
            device_id=dev, device_id_type=pl.DeviceIdType.MESH,
        )

    def twin_copy(plane):
        return moved(parts.at[plane, pl.ds((1 - core) * 2, 2)], twin_in, twin_send, twin_recv, twin_dev, plane)

    def cross_copy(plane):
        return moved(cross_out.at[plane], cross_in, cross_send, cross_recv, cross_dev, plane)

    def up_copy(plane, piece):
        return moved(line_out.at[plane, piece], line_up, up_send, up_recv, up_dev, (plane, piece))

    def down_copy(plane, piece):
        return moved(line_out.at[plane, piece], line_down, down_send, down_recv, down_dev, (plane, piece))

    def late_copy():
        return pltpu.make_async_remote_copy(
            src_ref=late_out, dst_ref=late_in, send_sem=late_sem.at[0], recv_sem=late_sem.at[1],
            device_id=cross_dev, device_id_type=pl.DeviceIdType.MESH,
        )

    def plane_of(i):
        second = jnp.where(z == 0, 1, z - 1)
        third = jnp.where(z == 0, 2, jnp.where(z == 3, 1, z + 1))
        fourth = jnp.where(z <= 1, 3, 0)
        return jnp.where(i == 0, z, jnp.where(i == 1, second, jnp.where(i == 2, third, fourth)))

    @pl.when(has_up)
    def _():
        block_copy(UP, z, own_slot).start()

    @pl.when(has_down)
    def _():
        block_copy(DOWN, z, own_slot).start()

    block_copy(ACROSS, z, own_slot).start()
    block_copy(TWIN, z, own_slot).start()

    def shift_in(dist):
        @pl.when(z - dist >= 0)
        def _():
            plane = jnp.maximum(z - dist, 0)
            block_copy(UP, plane, own_slot).wait_recv()

            @pl.when(has_up)
            def _():
                block_copy(UP, plane, own_slot).start()

            block_copy(ACROSS, plane, own_slot).start()
            block_copy(TWIN, plane, own_slot).start()

        @pl.when(z + dist <= length - 1)
        def _():
            plane = jnp.minimum(z + dist, length - 1)
            block_copy(DOWN, plane, own_slot).wait_recv()

            @pl.when(has_down)
            def _():
                block_copy(DOWN, plane, own_slot).start()

            block_copy(ACROSS, plane, own_slot).start()
            block_copy(TWIN, plane, own_slot).start()

    def expert_part(plane):
        group = rows[plane].reshape(4 * tok, rows_ref.shape[1])
        lane = lax.broadcasted_iota(jnp.int32, (4 * tok, 128), 1)
        first = width - spare + expert
        mine = (lane == first) | (lane == first + experts_all) | (lane == first + 2 * experts_all)
        tail = rows[plane, :, :, pl.ds(spare, 128)].reshape(4 * tok, 128).astype(jnp.float32)
        gain = jnp.sum(jnp.where(mine, tail, 0.0), axis=1, keepdims=True)
        group = group[:, :width]
        over = (((1,), (1,)), ((), ()))
        gate_proj = lax.dot_general(group, inner[0], over, preferred_element_type=jnp.float32)
        up_proj = lax.dot_general(group, inner[1], over, preferred_element_type=jnp.float32)
        hidden = ((up_proj + 1.0) * gate_proj * jax.nn.sigmoid(1.702 * gate_proj)).astype(jnp.bfloat16)
        for low in range(0, width, 1024):
            high = min(low + 1024, width)
            value = jnp.dot(hidden, outer[:, low:high], preferred_element_type=jnp.float32) * gain
            parts[plane, :, :, low:high] = value.astype(jnp.bfloat16).reshape(4, tok, high - low)

    near, far = slice(0, half), slice(half, tok)

    def pair_sum(plane, slot, source, span):
        return parts[plane, slot, span].astype(jnp.float32) + twin_in[plane, source, span].astype(jnp.float32)

    def cross_sum(plane):
        twin_copy(plane).wait_recv()
        cross_out[plane] = pair_sum(plane, cross_slot, 1 - x, near).astype(jnp.bfloat16)
        cross_copy(plane).start()

    def piece_sum(plane, piece):
        if piece == 1:
            return pair_sum(plane, cross_slot, 1 - x, far)
        if piece == 2:
            return pair_sum(plane, own_slot, x, far)
        cross_copy(plane).wait_recv()
        return pair_sum(plane, own_slot, x, near) + cross_in[plane].astype(jnp.float32)

    def line_first(plane, piece):
        line_out[plane, piece] = piece_sum(plane, piece).astype(jnp.bfloat16)

        @pl.when(z == 0)
        def _():
            up_copy(plane, piece).start()

        @pl.when(z == length - 1)
        def _():
            down_copy(plane, piece).start()

    def line_next(plane, piece):
        total = piece_sum(plane, piece)

        @pl.when(plane > z)
        def _():
            up_copy(plane, piece).wait_recv()
            line_out[plane, piece] = (total + line_up[plane, piece].astype(jnp.float32)).astype(jnp.bfloat16)
            up_copy(plane, piece).start()

        @pl.when(plane < z)
        def _():
            down_copy(plane, piece).wait_recv()
            line_out[plane, piece] = (total + line_down[plane, piece].astype(jnp.float32)).astype(jnp.bfloat16)
            down_copy(plane, piece).start()

    def step(i, carry):
        plane = plane_of(i)

        @pl.when(i < length - 1)
        def _():
            shift_in(i + 1)

        block_copy(ACROSS, plane, cross_slot).wait_recv()
        block_copy(TWIN, plane, cross_slot).start()
        for other in range(2):
            block_copy(TWIN, plane, (1 - core) * 2 + other).wait_recv()

        @pl.when(i == 0)
        def _():
            load_inner.wait()
            load_outer.wait()

        expert_part(plane)
        twin_copy(plane).start()

        cross_sum(plane)

        @pl.when(at_end & (i >= 1))
        def _():
            line_first(plane, 1)
            line_first(plane, 2)

        @pl.when(at_end & (i >= 2))
        def _():
            line_first(plane_of(i - 1), 0)

        return carry

    lax.fori_loop(0, length, step, 0)

    @pl.when(at_end)
    def _():
        line_first(plane_of(length - 1), 0)

    def line_step(j, carry):
        first = jnp.where(z <= 1, 2, 1)
        second = jnp.where(z <= 1, 3, 0)
        third = jnp.where(z <= 1, 0, 3)
        plane = jnp.where(j == 0, first, jnp.where(j == 1, second, third))
        for piece in (1, 2, 0):
            line_next(plane, piece)
        return carry

    @pl.when(jnp.logical_not(at_end))
    def _():
        lax.fori_loop(0, length - 1, line_step, 0)

    def arrived(piece):
        @pl.when(has_down)
        def _():
            up_copy(z, piece).wait_recv()

        @pl.when(has_up)
        def _():
            down_copy(z, piece).wait_recv()

        from_below = jnp.where(has_down, line_up[z, piece].astype(jnp.float32), 0.0)
        from_above = jnp.where(has_up, line_down[z, piece].astype(jnp.float32), 0.0)
        return piece_sum(z, piece) + from_below + from_above

    @pl.when(z == 0)
    def _():
        line_up[z] = jnp.zeros(line_up.shape[1:], jnp.bfloat16)

    @pl.when(z == length - 1)
    def _():
        line_down[z] = jnp.zeros(line_down.shape[1:], jnp.bfloat16)

    late_out[...] = arrived(1).astype(jnp.bfloat16)
    late_copy().start()
    out_ref[near] = arrived(0).astype(jnp.bfloat16)
    own = arrived(2)
    late_copy().wait_recv()
    out_ref[far] = (own + late_in[...].astype(jnp.float32)).astype(jnp.bfloat16)
    late_copy().wait_send()

    def drain(plane, carry):
        @pl.when(has_up & (plane <= z))
        def _():
            block_copy(UP, plane, own_slot).wait_send()

        @pl.when(has_down & (plane >= z))
        def _():
            block_copy(DOWN, plane, own_slot).wait_send()

        block_copy(ACROSS, plane, own_slot).wait_send()
        block_copy(TWIN, plane, own_slot).wait_send()
        block_copy(TWIN, plane, cross_slot).wait_send()
        twin_copy(plane).wait_send()
        cross_copy(plane).wait_send()

        @pl.when(plane > z)
        def _():
            for piece in range(3):
                up_copy(plane, piece).wait_send()

        @pl.when(plane < z)
        def _():
            for piece in range(3):
                down_copy(plane, piece).wait_send()

        return carry

    lax.fori_loop(0, length, drain, 0)


def line_body(activations, expert_ids, route_gates, inner_weight, outer_weight):
    tok, width = activations.shape
    hidden = outer_weight.shape[1]
    length = lax.axis_size("helper")
    experts_all = lax.axis_size("expert") * length // 2
    named = expert_ids[:, :, None] == jnp.arange(experts_all, dtype=jnp.int32)[None, None, :]
    weights = jnp.sum(jnp.where(named, route_gates[:, :, None], 0.0), axis=1)
    high = lax.reduce_precision(weights, 8, 7)
    middle = lax.reduce_precision(weights - high, 8, 7)
    low = weights - high - middle
    gates = jnp.concatenate([high, middle, low], axis=1).astype(jnp.bfloat16)
    whole = -(-width // 128) * 128
    rows = jnp.concatenate([activations, jnp.pad(gates, ((0, 0), (0, whole - width - gates.shape[1])))], axis=1)
    inner = jnp.swapaxes(inner_weight[0], 1, 2)
    bf16 = jnp.bfloat16
    dma = pltpu.SemaphoreType.DMA
    half = tok // 2
    halves = pltpu.VMEM((length, half, width), bf16)
    line = pltpu.VMEM((length, 3, half, width), bf16)
    return pl.pallas_call(
        line_kernel,
        out_shape=jax.ShapeDtypeStruct((tok, width), bf16),
        in_specs=[
            pl.BlockSpec(memory_space=pltpu.VMEM),
            pl.BlockSpec(memory_space=pl.ANY),
            pl.BlockSpec(memory_space=pl.ANY),
        ],
        out_specs=pl.BlockSpec(memory_space=pltpu.VMEM),
        scratch_shapes=[
            pltpu.VMEM((length, 4, tok, whole), bf16),
            pltpu.VMEM((2, hidden, width), bf16),
            pltpu.VMEM((hidden, width), bf16),
            pltpu.VMEM((length, 4, tok, width), bf16),
            pltpu.VMEM((length, 2, tok, width), bf16),
            halves, halves, line, line, line,
            dma((4, length, 4)), dma((length, 4)),
            dma((length,)), dma((length,)), dma((length,)), dma((length,)),
            pltpu.VMEM((half, width), bf16), pltpu.VMEM((half, width), bf16), dma((2,)),
            dma((length, 3)), dma((length, 3)), dma((length, 3)), dma((length, 3)),
            dma((2,)),
        ],
        compiler_params=pltpu.CompilerParams(
            collective_id=0, has_side_effects=True, vmem_limit_bytes=58 * 1024 * 1024
        ),
    )(rows, inner, outer_weight[0])


def body(activations, expert_ids, route_gates, inner_weight, outer_weight):
    tok_count, top_count = expert_ids.shape
    experts_all = lax.axis_size("expert") * lax.axis_size("helper") // 2
    capacity = 2 * max(1, tok_count * top_count // experts_all)
    spare = -activations.shape[1] % 128
    four = lax.axis_size("expert") == 4 and lax.axis_size("helper") == 4
    if capacity < tok_count:
        chosen = routed_body
    elif four and tok_count % 32 == 0 and spare >= 3 * experts_all:
        chosen = line_body
    else:
        chosen = dense_body
    return chosen(activations, expert_ids, route_gates, inner_weight, outer_weight)


def solution(mesh):
    placed = (
        P(("groups", "expert", "helper"), None),
        P(("groups", "expert", "helper"), None),
        P(("groups", "expert", "helper"), None),
        P(("expert", "helper"), None, None, None),
        P(("expert", "helper"), None, None),
    )
    return jax.shard_map(
        body,
        mesh=mesh,
        in_specs=placed,
        out_specs=P(("groups", "expert", "helper"), None),
        check_vma=False,
    )
```

```python
import jax
import jax.numpy as jnp
from jax import lax
from jax.experimental import pallas as pl
from jax.experimental.pallas import tpu as pltpu
from jax.sharding import PartitionSpec as P


def swapped(shard, axis, bit):
    return lax.ppermute(shard, axis, [(i, i ^ 1 << bit) for i in range(lax.axis_size(axis))])


def deliver(outgoing):
    return lax.all_to_all(outgoing, ("expert", "helper"), split_axis=0, concat_axis=0, tiled=True)


def send_back(outgoing):
    return lax.all_to_all(outgoing, ("expert", "helper"), split_axis=0, concat_axis=0, tiled=True)


def routed_body(activations, expert_ids, route_gates, inner_weight, outer_weight):
    tok_count, model_width = activations.shape
    top_count = expert_ids.shape[1]
    devices_all = lax.axis_size("expert") * lax.axis_size("helper")
    experts_all = devices_all // 2
    capacity = 2 * max(1, tok_count * top_count // experts_all)
    half_cap = capacity // 2
    flat_ids = expert_ids.reshape(-1)
    onehot = (flat_ids[:, None] == jnp.arange(experts_all, dtype=jnp.int32)[None, :]).astype(
        jnp.int32
    )
    ranking = jnp.sum(jnp.cumsum(onehot, axis=0) * onehot, axis=1) - 1
    slot_index = flat_ids * capacity + ranking
    token_index = jnp.arange(flat_ids.shape[0], dtype=jnp.int32) // top_count
    buffer = jnp.zeros((experts_all * capacity, model_width), activations.dtype)
    buffer = buffer.at[slot_index].set(activations[token_index])
    parity = lax.axis_index("helper") % 2
    arrived = deliver(jnp.repeat(buffer.reshape(experts_all, capacity, model_width), 2, axis=0))
    slot_rows = arrived.reshape(-1, model_width)
    projected = jnp.einsum(
        "rd,cdf->crf", slot_rows, inner_weight[0], preferred_element_type=jnp.float32
    )
    gate_proj = projected[0]
    up_proj = projected[1]
    hidden = ((up_proj + 1.0) * gate_proj * jax.nn.sigmoid(1.702 * gate_proj)).astype(jnp.bfloat16)
    partial_value = jnp.dot(hidden, outer_weight[0], preferred_element_type=jnp.float32).astype(
        jnp.bfloat16
    )
    partial_value = partial_value.reshape(devices_all, capacity, model_width)
    first_part = partial_value[:, :half_cap]
    second_part = partial_value[:, half_cap:]
    kept_half = jnp.where(parity == 0, first_part, second_part)
    given_half = jnp.where(parity == 0, second_part, first_part)
    received_half = swapped(given_half, "helper", 0)
    kept_half = lax.optimization_barrier(kept_half)
    summed = kept_half.astype(jnp.float32) + received_half.astype(jnp.float32)
    results = summed.astype(jnp.bfloat16)
    returned = send_back(results).reshape(experts_all * capacity, model_width)
    picked = returned[slot_index].astype(jnp.float32).reshape(tok_count, top_count, model_width)
    combined = jnp.sum(picked * route_gates[:, :, None], axis=1)
    return combined.astype(jnp.bfloat16)


AXES = ("expert", "helper")


def dense_body(activations, expert_ids, route_gates, inner_weight, outer_weight):
    experts_all = lax.axis_size("expert") * lax.axis_size("helper") // 2
    expert = (lax.axis_index("expert") * lax.axis_size("helper") + lax.axis_index("helper")) // 2
    named = expert_ids[:, :, None] == jnp.arange(experts_all, dtype=jnp.int32)[None, None, :]
    weights = jnp.sum(jnp.where(named, route_gates[:, :, None], 0.0), axis=1)
    rows = lax.all_gather(activations, AXES, axis=0, tiled=True)
    weights = lax.all_gather(weights, AXES, axis=0, tiled=True)
    own = jnp.sum(jnp.where(jnp.arange(experts_all)[None, :] == expert, weights, 0.0), axis=1)
    gate_proj = jnp.dot(rows, inner_weight[0, 0], preferred_element_type=jnp.float32)
    up_proj = jnp.dot(rows, inner_weight[0, 1], preferred_element_type=jnp.float32)
    hidden = ((up_proj + 1.0) * gate_proj * jax.nn.sigmoid(1.702 * gate_proj)).astype(jnp.bfloat16)
    partial = jnp.dot(hidden, outer_weight[0], preferred_element_type=jnp.float32)
    partial = (partial * own[:, None]).astype(jnp.bfloat16)
    return lax.psum_scatter(partial, AXES, scatter_dimension=0, tiled=True)


UP, DOWN, ACROSS, TWIN = 0, 1, 2, 3


def line_kernel(
    rows_ref, inner_ref, outer_ref, out_ref,
    rows, inner, outer, parts, twin_in, cross_out, cross_in, line_out, line_up, line_down,
    gather_send, gather_recv, twin_send, twin_recv, cross_send, cross_recv, late_out, late_in, late_sem,
    up_send, up_recv, down_send, down_recv, weight_sem,
):
    length = 4
    tok, width = out_ref.shape
    me = lax.axis_index("expert")
    z = lax.axis_index("helper")
    x, core = me // 2, me % 2
    spare = rows_ref.shape[1] - 128
    experts_all = lax.axis_size("expert") * lax.axis_size("helper") // 2
    expert = (me * length + z) // 2
    up_dev = {"helper": jnp.minimum(z + 1, length - 1)}
    down_dev = {"helper": jnp.maximum(z - 1, 0)}
    cross_dev = {"expert": (1 - x) * 2 + core}
    twin_dev = {"expert": x * 2 + (1 - core)}
    devs = (up_dev, down_dev, cross_dev, twin_dev)
    has_up, has_down = z < length - 1, z > 0
    at_end = (z == 0) | (z == length - 1)
    half = tok // 2
    nearest = jnp.where(z <= 1, 2, 1)
    own_slot = core * 2 + x
    cross_slot = core * 2 + (1 - x)

    load_inner = pltpu.make_async_copy(inner_ref, inner, weight_sem.at[0])
    load_outer = pltpu.make_async_copy(outer_ref, outer, weight_sem.at[1])
    load_inner.start()
    load_outer.start()

    barrier = pltpu.get_barrier_semaphore()

    def greet(dev):
        pl.semaphore_signal(barrier, inc=1, device_id=dev, device_id_type=pl.DeviceIdType.MESH)

    greet(cross_dev)
    greet(twin_dev)

    @pl.when(has_up)
    def _():
        greet(up_dev)

    @pl.when(has_down)
    def _():
        greet(down_dev)

    rows[z, own_slot] = rows_ref[...]
    pl.semaphore_wait(barrier, jnp.where(has_up & has_down, 4, 3))

    def block_copy(way, plane, slot):
        return pltpu.make_async_remote_copy(
            src_ref=rows.at[plane, slot], dst_ref=rows.at[plane, slot],
            send_sem=gather_send.at[way, plane, slot], recv_sem=gather_recv.at[plane, slot],
            device_id=devs[way], device_id_type=pl.DeviceIdType.MESH,
        )

    def sem_at(ref, at):
        return ref.at[at[0], at[1]] if isinstance(at, tuple) else ref.at[at]

    def moved(src, dst, send, recv, dev, at):
        return pltpu.make_async_remote_copy(
            src_ref=src, dst_ref=sem_at(dst, at), send_sem=sem_at(send, at), recv_sem=sem_at(recv, at),
            device_id=dev, device_id_type=pl.DeviceIdType.MESH,
        )

    def twin_copy(plane):
        return moved(parts.at[plane, pl.ds((1 - core) * 2, 2)], twin_in, twin_send, twin_recv, twin_dev, plane)

    def cross_copy(plane):
        return moved(cross_out.at[plane], cross_in, cross_send, cross_recv, cross_dev, plane)

    def up_copy(plane, piece):
        return moved(line_out.at[plane, piece], line_up, up_send, up_recv, up_dev, (plane, piece))

    def down_copy(plane, piece):
        return moved(line_out.at[plane, piece], line_down, down_send, down_recv, down_dev, (plane, piece))

    def late_copy():
        return pltpu.make_async_remote_copy(
            src_ref=late_out, dst_ref=late_in, send_sem=late_sem.at[0], recv_sem=late_sem.at[1],
            device_id=cross_dev, device_id_type=pl.DeviceIdType.MESH,
        )

    def plane_of(i):
        second = jnp.where(z == 0, 1, z - 1)
        third = jnp.where(z == 0, 2, jnp.where(z == 3, 1, z + 1))
        fourth = jnp.where(z <= 1, 3, 0)
        return jnp.where(i == 0, z, jnp.where(i == 1, second, jnp.where(i == 2, third, fourth)))

    @pl.when(has_up)
    def _():
        block_copy(UP, z, own_slot).start()

    @pl.when(has_down)
    def _():
        block_copy(DOWN, z, own_slot).start()

    block_copy(ACROSS, z, own_slot).start()
    block_copy(TWIN, z, own_slot).start()

    def shift_in(dist):
        @pl.when(z - dist >= 0)
        def _():
            plane = jnp.maximum(z - dist, 0)
            block_copy(UP, plane, own_slot).wait_recv()

            @pl.when(has_up)
            def _():
                block_copy(UP, plane, own_slot).start()

            block_copy(ACROSS, plane, own_slot).start()
            block_copy(TWIN, plane, own_slot).start()

        @pl.when(z + dist <= length - 1)
        def _():
            plane = jnp.minimum(z + dist, length - 1)
            block_copy(DOWN, plane, own_slot).wait_recv()

            @pl.when(has_down)
            def _():
                block_copy(DOWN, plane, own_slot).start()

            block_copy(ACROSS, plane, own_slot).start()
            block_copy(TWIN, plane, own_slot).start()

    def expert_part(plane):
        group = rows[plane].reshape(4 * tok, rows_ref.shape[1])
        lane = lax.broadcasted_iota(jnp.int32, (4 * tok, 128), 1)
        first = width - spare + expert
        mine = (lane == first) | (lane == first + experts_all) | (lane == first + 2 * experts_all)
        tail = rows[plane, :, :, pl.ds(spare, 128)].reshape(4 * tok, 128).astype(jnp.float32)
        gain = jnp.sum(jnp.where(mine, tail, 0.0), axis=1, keepdims=True)
        group = group[:, :width]
        over = (((1,), (1,)), ((), ()))
        gate_proj = lax.dot_general(group, inner[0], over, preferred_element_type=jnp.float32)
        up_proj = lax.dot_general(group, inner[1], over, preferred_element_type=jnp.float32)
        hidden = ((up_proj + 1.0) * gate_proj * jax.nn.sigmoid(1.702 * gate_proj)).astype(jnp.bfloat16)
        for low in range(0, width, 1024):
            high = min(low + 1024, width)
            value = jnp.dot(hidden, outer[:, low:high], preferred_element_type=jnp.float32) * gain
            parts[plane, :, :, low:high] = value.astype(jnp.bfloat16).reshape(4, tok, high - low)

    near, far = slice(0, half), slice(half, tok)

    def pair_sum(plane, slot, source, span):
        return parts[plane, slot, span].astype(jnp.float32) + twin_in[plane, source, span].astype(jnp.float32)

    def cross_sum(plane):
        twin_copy(plane).wait_recv()
        cross_out[plane] = pair_sum(plane, cross_slot, 1 - x, near).astype(jnp.bfloat16)
        cross_copy(plane).start()

    def piece_sum(plane, piece):
        if piece == 1:
            return pair_sum(plane, cross_slot, 1 - x, far)
        if piece == 2:
            return pair_sum(plane, own_slot, x, far)
        cross_copy(plane).wait_recv()
        return pair_sum(plane, own_slot, x, near) + cross_in[plane].astype(jnp.float32)

    def line_first(plane, piece):
        line_out[plane, piece] = piece_sum(plane, piece).astype(jnp.bfloat16)

        @pl.when(z == 0)
        def _():
            up_copy(plane, piece).start()

        @pl.when(z == length - 1)
        def _():
            down_copy(plane, piece).start()

    def line_next(plane, piece):
        total = piece_sum(plane, piece)

        @pl.when(plane > z)
        def _():
            up_copy(plane, piece).wait_recv()
            line_out[plane, piece] = (total + line_up[plane, piece].astype(jnp.float32)).astype(jnp.bfloat16)
            up_copy(plane, piece).start()

        @pl.when(plane < z)
        def _():
            down_copy(plane, piece).wait_recv()
            line_out[plane, piece] = (total + line_down[plane, piece].astype(jnp.float32)).astype(jnp.bfloat16)
            down_copy(plane, piece).start()

    def step(i, carry):
        plane = plane_of(i)

        @pl.when(i < length - 1)
        def _():
            shift_in(i + 1)

        block_copy(ACROSS, plane, cross_slot).wait_recv()
        block_copy(TWIN, plane, cross_slot).start()

        @pl.when(jnp.logical_not(at_end) & (i == length - 1))
        def _():
            line_next(nearest, 1)
            line_next(nearest, 2)

        for other in range(2):
            block_copy(TWIN, plane, (1 - core) * 2 + other).wait_recv()

        @pl.when(i == 0)
        def _():
            load_inner.wait()
            load_outer.wait()

        expert_part(plane)
        twin_copy(plane).start()

        @pl.when(i >= 1)
        def _():
            cross_sum(plane)

        @pl.when(at_end & (i >= 1))
        def _():
            line_first(plane, 1)
            line_first(plane, 2)

        @pl.when(at_end & (i >= 2))
        def _():
            line_first(plane_of(i - 1), 0)

        return carry

    lax.fori_loop(0, length, step, 0)
    cross_sum(z)

    @pl.when(at_end)
    def _():
        line_first(plane_of(length - 1), 0)

    def line_step(j, carry):
        plane = jnp.where((z <= 1) == (j == 0), 3, 0)
        for piece in (1, 2, 0):
            line_next(plane, piece)
        return carry

    @pl.when(jnp.logical_not(at_end))
    def _():
        line_next(nearest, 0)
        lax.fori_loop(0, 2, line_step, 0)

    def arrived(piece):
        @pl.when(has_down)
        def _():
            up_copy(z, piece).wait_recv()

        @pl.when(has_up)
        def _():
            down_copy(z, piece).wait_recv()

        from_below = jnp.where(has_down, line_up[z, piece].astype(jnp.float32), 0.0)
        from_above = jnp.where(has_up, line_down[z, piece].astype(jnp.float32), 0.0)
        return piece_sum(z, piece) + from_below + from_above

    @pl.when(z == 0)
    def _():
        line_up[z] = jnp.zeros(line_up.shape[1:], jnp.bfloat16)

    @pl.when(z == length - 1)
    def _():
        line_down[z] = jnp.zeros(line_down.shape[1:], jnp.bfloat16)

    late_out[...] = arrived(1).astype(jnp.bfloat16)
    late_copy().start()
    out_ref[near] = arrived(0).astype(jnp.bfloat16)
    own = arrived(2)
    late_copy().wait_recv()
    out_ref[far] = (own + late_in[...].astype(jnp.float32)).astype(jnp.bfloat16)
    late_copy().wait_send()

    def drain(plane, carry):
        @pl.when(has_up & (plane <= z))
        def _():
            block_copy(UP, plane, own_slot).wait_send()

        @pl.when(has_down & (plane >= z))
        def _():
            block_copy(DOWN, plane, own_slot).wait_send()

        block_copy(ACROSS, plane, own_slot).wait_send()
        block_copy(TWIN, plane, own_slot).wait_send()
        block_copy(TWIN, plane, cross_slot).wait_send()
        twin_copy(plane).wait_send()
        cross_copy(plane).wait_send()

        @pl.when(plane > z)
        def _():
            for piece in range(3):
                up_copy(plane, piece).wait_send()

        @pl.when(plane < z)
        def _():
            for piece in range(3):
                down_copy(plane, piece).wait_send()

        return carry

    lax.fori_loop(0, length, drain, 0)


def line_body(activations, expert_ids, route_gates, inner_weight, outer_weight):
    tok, width = activations.shape
    hidden = outer_weight.shape[1]
    length = lax.axis_size("helper")
    experts_all = lax.axis_size("expert") * length // 2
    named = expert_ids[:, :, None] == jnp.arange(experts_all, dtype=jnp.int32)[None, None, :]
    weights = jnp.sum(jnp.where(named, route_gates[:, :, None], 0.0), axis=1)
    high = lax.reduce_precision(weights, 8, 7)
    middle = lax.reduce_precision(weights - high, 8, 7)
    low = weights - high - middle
    gates = jnp.concatenate([high, middle, low], axis=1).astype(jnp.bfloat16)
    whole = -(-width // 128) * 128
    rows = jnp.concatenate([activations, jnp.pad(gates, ((0, 0), (0, whole - width - gates.shape[1])))], axis=1)
    inner = jnp.swapaxes(inner_weight[0], 1, 2)
    bf16 = jnp.bfloat16
    dma = pltpu.SemaphoreType.DMA
    half = tok // 2
    halves = pltpu.VMEM((length, half, width), bf16)
    line = pltpu.VMEM((length, 3, half, width), bf16)
    return pl.pallas_call(
        line_kernel,
        out_shape=jax.ShapeDtypeStruct((tok, width), bf16),
        in_specs=[
            pl.BlockSpec(memory_space=pltpu.VMEM),
            pl.BlockSpec(memory_space=pl.ANY),
            pl.BlockSpec(memory_space=pl.ANY),
        ],
        out_specs=pl.BlockSpec(memory_space=pltpu.VMEM),
        scratch_shapes=[
            pltpu.VMEM((length, 4, tok, whole), bf16),
            pltpu.VMEM((2, hidden, width), bf16),
            pltpu.VMEM((hidden, width), bf16),
            pltpu.VMEM((length, 4, tok, width), bf16),
            pltpu.VMEM((length, 2, tok, width), bf16),
            halves, halves, line, line, line,
            dma((4, length, 4)), dma((length, 4)),
            dma((length,)), dma((length,)), dma((length,)), dma((length,)),
            pltpu.VMEM((half, width), bf16), pltpu.VMEM((half, width), bf16), dma((2,)),
            dma((length, 3)), dma((length, 3)), dma((length, 3)), dma((length, 3)),
            dma((2,)),
        ],
        compiler_params=pltpu.CompilerParams(
            collective_id=0, has_side_effects=True, vmem_limit_bytes=58 * 1024 * 1024
        ),
    )(rows, inner, outer_weight[0])


def body(activations, expert_ids, route_gates, inner_weight, outer_weight):
    tok_count, top_count = expert_ids.shape
    experts_all = lax.axis_size("expert") * lax.axis_size("helper") // 2
    capacity = 2 * max(1, tok_count * top_count // experts_all)
    spare = -activations.shape[1] % 128
    four = lax.axis_size("expert") == 4 and lax.axis_size("helper") == 4
    if capacity < tok_count:
        chosen = routed_body
    elif four and tok_count % 32 == 0 and spare >= 3 * experts_all:
        chosen = line_body
    else:
        chosen = dense_body
    return chosen(activations, expert_ids, route_gates, inner_weight, outer_weight)


def solution(mesh):
    placed = (
        P(("groups", "expert", "helper"), None),
        P(("groups", "expert", "helper"), None),
        P(("groups", "expert", "helper"), None),
        P(("expert", "helper"), None, None, None),
        P(("expert", "helper"), None, None),
    )
    return jax.shard_map(
        body,
        mesh=mesh,
        in_specs=placed,
        out_specs=P(("groups", "expert", "helper"), None),
        check_vma=False,
    )
```

```python
import jax
import jax.numpy as jnp
from jax import lax
from jax.experimental import pallas as pl
from jax.experimental.pallas import tpu as pltpu
from jax.sharding import PartitionSpec as P


def swapped(shard, axis, bit):
    return lax.ppermute(shard, axis, [(i, i ^ 1 << bit) for i in range(lax.axis_size(axis))])


def deliver(outgoing):
    return lax.all_to_all(outgoing, ("expert", "helper"), split_axis=0, concat_axis=0, tiled=True)


def send_back(outgoing):
    return lax.all_to_all(outgoing, ("expert", "helper"), split_axis=0, concat_axis=0, tiled=True)


def routed_body(activations, expert_ids, route_gates, inner_weight, outer_weight):
    tok_count, model_width = activations.shape
    top_count = expert_ids.shape[1]
    devices_all = lax.axis_size("expert") * lax.axis_size("helper")
    experts_all = devices_all // 2
    capacity = 2 * max(1, tok_count * top_count // experts_all)
    half_cap = capacity // 2
    flat_ids = expert_ids.reshape(-1)
    onehot = (flat_ids[:, None] == jnp.arange(experts_all, dtype=jnp.int32)[None, :]).astype(
        jnp.int32
    )
    ranking = jnp.sum(jnp.cumsum(onehot, axis=0) * onehot, axis=1) - 1
    slot_index = flat_ids * capacity + ranking
    token_index = jnp.arange(flat_ids.shape[0], dtype=jnp.int32) // top_count
    buffer = jnp.zeros((experts_all * capacity, model_width), activations.dtype)
    buffer = buffer.at[slot_index].set(activations[token_index])
    parity = lax.axis_index("helper") % 2
    arrived = deliver(jnp.repeat(buffer.reshape(experts_all, capacity, model_width), 2, axis=0))
    slot_rows = arrived.reshape(-1, model_width)
    projected = jnp.einsum(
        "rd,cdf->crf", slot_rows, inner_weight[0], preferred_element_type=jnp.float32
    )
    gate_proj = projected[0]
    up_proj = projected[1]
    hidden = ((up_proj + 1.0) * gate_proj * jax.nn.sigmoid(1.702 * gate_proj)).astype(jnp.bfloat16)
    partial_value = jnp.dot(hidden, outer_weight[0], preferred_element_type=jnp.float32).astype(
        jnp.bfloat16
    )
    partial_value = partial_value.reshape(devices_all, capacity, model_width)
    first_part = partial_value[:, :half_cap]
    second_part = partial_value[:, half_cap:]
    kept_half = jnp.where(parity == 0, first_part, second_part)
    given_half = jnp.where(parity == 0, second_part, first_part)
    received_half = swapped(given_half, "helper", 0)
    kept_half = lax.optimization_barrier(kept_half)
    summed = kept_half.astype(jnp.float32) + received_half.astype(jnp.float32)
    results = summed.astype(jnp.bfloat16)
    returned = send_back(results).reshape(experts_all * capacity, model_width)
    picked = returned[slot_index].astype(jnp.float32).reshape(tok_count, top_count, model_width)
    combined = jnp.sum(picked * route_gates[:, :, None], axis=1)
    return combined.astype(jnp.bfloat16)


AXES = ("expert", "helper")


def dense_body(activations, expert_ids, route_gates, inner_weight, outer_weight):
    experts_all = lax.axis_size("expert") * lax.axis_size("helper") // 2
    expert = (lax.axis_index("expert") * lax.axis_size("helper") + lax.axis_index("helper")) // 2
    named = expert_ids[:, :, None] == jnp.arange(experts_all, dtype=jnp.int32)[None, None, :]
    weights = jnp.sum(jnp.where(named, route_gates[:, :, None], 0.0), axis=1)
    rows = lax.all_gather(activations, AXES, axis=0, tiled=True)
    weights = lax.all_gather(weights, AXES, axis=0, tiled=True)
    own = jnp.sum(jnp.where(jnp.arange(experts_all)[None, :] == expert, weights, 0.0), axis=1)
    gate_proj = jnp.dot(rows, inner_weight[0, 0], preferred_element_type=jnp.float32)
    up_proj = jnp.dot(rows, inner_weight[0, 1], preferred_element_type=jnp.float32)
    hidden = ((up_proj + 1.0) * gate_proj * jax.nn.sigmoid(1.702 * gate_proj)).astype(jnp.bfloat16)
    partial = jnp.dot(hidden, outer_weight[0], preferred_element_type=jnp.float32)
    partial = (partial * own[:, None]).astype(jnp.bfloat16)
    return lax.psum_scatter(partial, AXES, scatter_dimension=0, tiled=True)


UP, DOWN, ACROSS, TWIN = 0, 1, 2, 3


def line_kernel(
    rows_ref, inner_ref, outer_ref, out_ref,
    rows, inner, outer, parts, twin_in, cross_out, cross_in, line_out, line_up, line_down,
    gather_send, gather_recv, twin_send, twin_recv, cross_send, cross_recv, late_out, late_in, late_sem,
    tail_send, tail_recv,
    up_send, up_recv, down_send, down_recv, weight_sem,
):
    length = 4
    tok, width = out_ref.shape
    me = lax.axis_index("expert")
    z = lax.axis_index("helper")
    x, core = me // 2, me % 2
    spare = rows_ref.shape[1] - 128
    experts_all = lax.axis_size("expert") * lax.axis_size("helper") // 2
    expert = (me * length + z) // 2
    up_dev = {"helper": jnp.minimum(z + 1, length - 1)}
    down_dev = {"helper": jnp.maximum(z - 1, 0)}
    cross_dev = {"expert": (1 - x) * 2 + core}
    twin_dev = {"expert": x * 2 + (1 - core)}
    devs = (up_dev, down_dev, cross_dev, twin_dev)
    has_up, has_down = z < length - 1, z > 0
    at_end = (z == 0) | (z == length - 1)
    half = tok // 2
    nearest = jnp.where(z <= 1, 2, 1)
    own_slot = core * 2 + x
    cross_slot = core * 2 + (1 - x)

    load_inner = pltpu.make_async_copy(inner_ref, inner, weight_sem.at[0])
    load_outer = pltpu.make_async_copy(outer_ref, outer, weight_sem.at[1])
    load_inner.start()
    load_outer.start()

    barrier = pltpu.get_barrier_semaphore()

    def greet(dev):
        pl.semaphore_signal(barrier, inc=1, device_id=dev, device_id_type=pl.DeviceIdType.MESH)

    greet(cross_dev)
    greet(twin_dev)

    @pl.when(has_up)
    def _():
        greet(up_dev)

    @pl.when(has_down)
    def _():
        greet(down_dev)

    rows[z, own_slot] = rows_ref[...]
    pl.semaphore_wait(barrier, jnp.where(has_up & has_down, 4, 3))

    def block_copy(way, plane, slot):
        return pltpu.make_async_remote_copy(
            src_ref=rows.at[plane, slot], dst_ref=rows.at[plane, slot],
            send_sem=gather_send.at[way, plane, slot], recv_sem=gather_recv.at[plane, slot],
            device_id=devs[way], device_id_type=pl.DeviceIdType.MESH,
        )

    def sem_at(ref, at):
        return ref.at[at[0], at[1]] if isinstance(at, tuple) else ref.at[at]

    main = tok - 16

    def main_copy(plane, slot):
        return pltpu.make_async_remote_copy(
            src_ref=rows.at[plane, slot, pl.ds(0, main)], dst_ref=rows.at[plane, slot, pl.ds(0, main)],
            send_sem=gather_send.at[ACROSS, plane, slot], recv_sem=gather_recv.at[plane, slot],
            device_id=cross_dev, device_id_type=pl.DeviceIdType.MESH,
        )

    def tail_copy(way, plane, slot):
        return pltpu.make_async_remote_copy(
            src_ref=rows.at[plane, slot, pl.ds(main, 16)], dst_ref=rows.at[plane, slot, pl.ds(main, 16)],
            send_sem=tail_send.at[way, plane], recv_sem=tail_recv.at[plane],
            device_id=devs[way], device_id_type=pl.DeviceIdType.MESH,
        )

    def moved(src, dst, send, recv, dev, at):
        return pltpu.make_async_remote_copy(
            src_ref=src, dst_ref=sem_at(dst, at), send_sem=sem_at(send, at), recv_sem=sem_at(recv, at),
            device_id=dev, device_id_type=pl.DeviceIdType.MESH,
        )

    def twin_copy(plane):
        return moved(parts.at[plane, pl.ds((1 - core) * 2, 2)], twin_in, twin_send, twin_recv, twin_dev, plane)

    def cross_copy(plane):
        return moved(cross_out.at[plane], cross_in, cross_send, cross_recv, cross_dev, plane)

    def up_copy(plane, piece):
        return moved(line_out.at[plane, piece], line_up, up_send, up_recv, up_dev, (plane, piece))

    def down_copy(plane, piece):
        return moved(line_out.at[plane, piece], line_down, down_send, down_recv, down_dev, (plane, piece))

    def late_copy():
        return pltpu.make_async_remote_copy(
            src_ref=late_out, dst_ref=late_in, send_sem=late_sem.at[0], recv_sem=late_sem.at[1],
            device_id=cross_dev, device_id_type=pl.DeviceIdType.MESH,
        )

    def plane_of(i):
        second = jnp.where(z == 0, 1, z - 1)
        third = jnp.where(z == 0, 2, jnp.where(z == 3, 1, z + 1))
        fourth = jnp.where(z <= 1, 3, 0)
        return jnp.where(i == 0, z, jnp.where(i == 1, second, jnp.where(i == 2, third, fourth)))

    @pl.when(has_up)
    def _():
        block_copy(UP, z, own_slot).start()

    @pl.when(has_down)
    def _():
        block_copy(DOWN, z, own_slot).start()

    tail_copy(ACROSS, z, own_slot).start()
    main_copy(z, own_slot).start()
    block_copy(TWIN, z, own_slot).start()
    tail_copy(ACROSS, z, cross_slot).wait_recv()

    @pl.when(has_up)
    def _():
        tail_copy(UP, z, cross_slot).start()

    @pl.when(has_down)
    def _():
        tail_copy(DOWN, z, cross_slot).start()

    def shift_in(dist):
        @pl.when(z - dist >= 0)
        def _():
            plane = jnp.maximum(z - dist, 0)
            block_copy(UP, plane, own_slot).wait_recv()

            @pl.when(has_up)
            def _():
                block_copy(UP, plane, own_slot).start()

            main_copy(plane, own_slot).start()
            block_copy(TWIN, plane, own_slot).start()
            tail_copy(UP, plane, cross_slot).wait_recv()

            @pl.when(has_up)
            def _():
                tail_copy(UP, plane, cross_slot).start()

        @pl.when(z + dist <= length - 1)
        def _():
            plane = jnp.minimum(z + dist, length - 1)
            block_copy(DOWN, plane, own_slot).wait_recv()

            @pl.when(has_down)
            def _():
                block_copy(DOWN, plane, own_slot).start()

            main_copy(plane, own_slot).start()
            block_copy(TWIN, plane, own_slot).start()
            tail_copy(DOWN, plane, cross_slot).wait_recv()

            @pl.when(has_down)
            def _():
                tail_copy(DOWN, plane, cross_slot).start()

    def expert_part(plane):
        group = rows[plane].reshape(4 * tok, rows_ref.shape[1])
        lane = lax.broadcasted_iota(jnp.int32, (4 * tok, 128), 1)
        first = width - spare + expert
        mine = (lane == first) | (lane == first + experts_all) | (lane == first + 2 * experts_all)
        tail = rows[plane, :, :, pl.ds(spare, 128)].reshape(4 * tok, 128).astype(jnp.float32)
        gain = jnp.sum(jnp.where(mine, tail, 0.0), axis=1, keepdims=True)
        group = group[:, :width]
        over = (((1,), (1,)), ((), ()))
        gate_proj = lax.dot_general(group, inner[0], over, preferred_element_type=jnp.float32)
        up_proj = lax.dot_general(group, inner[1], over, preferred_element_type=jnp.float32)
        hidden = ((up_proj + 1.0) * gate_proj * jax.nn.sigmoid(1.702 * gate_proj)).astype(jnp.bfloat16)
        for low in range(0, width, 1024):
            high = min(low + 1024, width)
            value = jnp.dot(hidden, outer[:, low:high], preferred_element_type=jnp.float32) * gain
            parts[plane, :, :, low:high] = value.astype(jnp.bfloat16).reshape(4, tok, high - low)

    near, far = slice(0, half), slice(half, tok)

    def pair_sum(plane, slot, source, span):
        return parts[plane, slot, span].astype(jnp.float32) + twin_in[plane, source, span].astype(jnp.float32)

    def cross_sum(plane):
        twin_copy(plane).wait_recv()
        cross_out[plane] = pair_sum(plane, cross_slot, 1 - x, near).astype(jnp.bfloat16)
        cross_copy(plane).start()

    def piece_sum(plane, piece):
        if piece == 1:
            return pair_sum(plane, cross_slot, 1 - x, far)
        if piece == 2:
            return pair_sum(plane, own_slot, x, far)
        cross_copy(plane).wait_recv()
        return pair_sum(plane, own_slot, x, near) + cross_in[plane].astype(jnp.float32)

    def line_first(plane, piece):
        line_out[plane, piece] = piece_sum(plane, piece).astype(jnp.bfloat16)

        @pl.when(z == 0)
        def _():
            up_copy(plane, piece).start()

        @pl.when(z == length - 1)
        def _():
            down_copy(plane, piece).start()

    def line_next(plane, piece):
        total = piece_sum(plane, piece)

        @pl.when(plane > z)
        def _():
            up_copy(plane, piece).wait_recv()
            line_out[plane, piece] = (total + line_up[plane, piece].astype(jnp.float32)).astype(jnp.bfloat16)
            up_copy(plane, piece).start()

        @pl.when(plane < z)
        def _():
            down_copy(plane, piece).wait_recv()
            line_out[plane, piece] = (total + line_down[plane, piece].astype(jnp.float32)).astype(jnp.bfloat16)
            down_copy(plane, piece).start()

    def step(i, carry):
        plane = plane_of(i)

        @pl.when(i < length - 1)
        def _():
            shift_in(i + 1)

        main_copy(plane, cross_slot).wait_recv()
        block_copy(TWIN, plane, cross_slot).start()

        @pl.when(jnp.logical_not(at_end) & (i == length - 1))
        def _():
            line_next(nearest, 1)
            line_next(nearest, 2)

        for other in range(2):
            block_copy(TWIN, plane, (1 - core) * 2 + other).wait_recv()

        @pl.when(i == 0)
        def _():
            load_inner.wait()
            load_outer.wait()

        expert_part(plane)
        twin_copy(plane).start()

        @pl.when(i >= 1)
        def _():
            cross_sum(plane)

        @pl.when(at_end & (i >= 1))
        def _():
            line_first(plane, 1)
            line_first(plane, 2)

        @pl.when(at_end & (i >= 2))
        def _():
            line_first(plane_of(i - 1), 0)

        return carry

    lax.fori_loop(0, length, step, 0)
    cross_sum(z)

    @pl.when(at_end)
    def _():
        line_first(plane_of(length - 1), 0)

    def line_step(j, carry):
        plane = jnp.where((z <= 1) == (j == 0), 3, 0)
        for piece in (1, 2, 0):
            line_next(plane, piece)
        return carry

    @pl.when(jnp.logical_not(at_end))
    def _():
        line_next(nearest, 0)
        lax.fori_loop(0, 2, line_step, 0)

    def arrived(piece):
        @pl.when(has_down)
        def _():
            up_copy(z, piece).wait_recv()

        @pl.when(has_up)
        def _():
            down_copy(z, piece).wait_recv()

        from_below = jnp.where(has_down, line_up[z, piece].astype(jnp.float32), 0.0)
        from_above = jnp.where(has_up, line_down[z, piece].astype(jnp.float32), 0.0)
        return piece_sum(z, piece) + from_below + from_above

    @pl.when(z == 0)
    def _():
        line_up[z] = jnp.zeros(line_up.shape[1:], jnp.bfloat16)

    @pl.when(z == length - 1)
    def _():
        line_down[z] = jnp.zeros(line_down.shape[1:], jnp.bfloat16)

    late_out[...] = arrived(1).astype(jnp.bfloat16)
    late_copy().start()
    out_ref[near] = arrived(0).astype(jnp.bfloat16)
    own = arrived(2)
    late_copy().wait_recv()
    out_ref[far] = (own + late_in[...].astype(jnp.float32)).astype(jnp.bfloat16)
    late_copy().wait_send()

    def drain(plane, carry):
        @pl.when(has_up & (plane <= z))
        def _():
            block_copy(UP, plane, own_slot).wait_send()

        @pl.when(has_down & (plane >= z))
        def _():
            block_copy(DOWN, plane, own_slot).wait_send()

        main_copy(plane, own_slot).wait_send()

        @pl.when(has_up & (plane <= z))
        def _():
            tail_copy(UP, plane, cross_slot).wait_send()

        @pl.when(has_down & (plane >= z))
        def _():
            tail_copy(DOWN, plane, cross_slot).wait_send()

        block_copy(TWIN, plane, own_slot).wait_send()
        block_copy(TWIN, plane, cross_slot).wait_send()
        twin_copy(plane).wait_send()
        cross_copy(plane).wait_send()

        @pl.when(plane > z)
        def _():
            for piece in range(3):
                up_copy(plane, piece).wait_send()

        @pl.when(plane < z)
        def _():
            for piece in range(3):
                down_copy(plane, piece).wait_send()

        return carry

    lax.fori_loop(0, length, drain, 0)
    tail_copy(ACROSS, z, own_slot).wait_send()


def line_body(activations, expert_ids, route_gates, inner_weight, outer_weight):
    tok, width = activations.shape
    hidden = outer_weight.shape[1]
    length = lax.axis_size("helper")
    experts_all = lax.axis_size("expert") * length // 2
    named = expert_ids[:, :, None] == jnp.arange(experts_all, dtype=jnp.int32)[None, None, :]
    weights = jnp.sum(jnp.where(named, route_gates[:, :, None], 0.0), axis=1)
    high = lax.reduce_precision(weights, 8, 7)
    middle = lax.reduce_precision(weights - high, 8, 7)
    low = weights - high - middle
    gates = jnp.concatenate([high, middle, low], axis=1).astype(jnp.bfloat16)
    whole = -(-width // 128) * 128
    rows = jnp.concatenate([activations, jnp.pad(gates, ((0, 0), (0, whole - width - gates.shape[1])))], axis=1)
    inner = jnp.swapaxes(inner_weight[0], 1, 2)
    bf16 = jnp.bfloat16
    dma = pltpu.SemaphoreType.DMA
    half = tok // 2
    halves = pltpu.VMEM((length, half, width), bf16)
    line = pltpu.VMEM((length, 3, half, width), bf16)
    return pl.pallas_call(
        line_kernel,
        out_shape=jax.ShapeDtypeStruct((tok, width), bf16),
        in_specs=[
            pl.BlockSpec(memory_space=pltpu.VMEM),
            pl.BlockSpec(memory_space=pl.ANY),
            pl.BlockSpec(memory_space=pl.ANY),
        ],
        out_specs=pl.BlockSpec(memory_space=pltpu.VMEM),
        scratch_shapes=[
            pltpu.VMEM((length, 4, tok, whole), bf16),
            pltpu.VMEM((2, hidden, width), bf16),
            pltpu.VMEM((hidden, width), bf16),
            pltpu.VMEM((length, 4, tok, width), bf16),
            pltpu.VMEM((length, 2, tok, width), bf16),
            halves, halves, line, line, line,
            dma((4, length, 4)), dma((length, 4)),
            dma((length,)), dma((length,)), dma((length,)), dma((length,)),
            pltpu.VMEM((half, width), bf16), pltpu.VMEM((half, width), bf16), dma((2,)),
            dma((3, length)), dma((length,)),
            dma((length, 3)), dma((length, 3)), dma((length, 3)), dma((length, 3)),
            dma((2,)),
        ],
        compiler_params=pltpu.CompilerParams(
            collective_id=0, has_side_effects=True, vmem_limit_bytes=58 * 1024 * 1024
        ),
    )(rows, inner, outer_weight[0])


def body(activations, expert_ids, route_gates, inner_weight, outer_weight):
    tok_count, top_count = expert_ids.shape
    experts_all = lax.axis_size("expert") * lax.axis_size("helper") // 2
    capacity = 2 * max(1, tok_count * top_count // experts_all)
    spare = -activations.shape[1] % 128
    four = lax.axis_size("expert") == 4 and lax.axis_size("helper") == 4
    if capacity < tok_count:
        chosen = routed_body
    elif four and tok_count % 32 == 0 and spare >= 3 * experts_all:
        chosen = line_body
    else:
        chosen = dense_body
    return chosen(activations, expert_ids, route_gates, inner_weight, outer_weight)


def solution(mesh):
    placed = (
        P(("groups", "expert", "helper"), None),
        P(("groups", "expert", "helper"), None),
        P(("groups", "expert", "helper"), None),
        P(("expert", "helper"), None, None, None),
        P(("expert", "helper"), None, None),
    )
    return jax.shard_map(
        body,
        mesh=mesh,
        in_specs=placed,
        out_specs=P(("groups", "expert", "helper"), None),
        check_vma=False,
    )
```

```python
import jax
import jax.numpy as jnp
from jax import lax
from jax.experimental import pallas as pl
from jax.experimental.pallas import tpu as pltpu
from jax.sharding import PartitionSpec as P


def swapped(shard, axis, bit):
    return lax.ppermute(shard, axis, [(i, i ^ 1 << bit) for i in range(lax.axis_size(axis))])


def deliver(outgoing):
    return lax.all_to_all(outgoing, ("expert", "helper"), split_axis=0, concat_axis=0, tiled=True)


def send_back(outgoing):
    return lax.all_to_all(outgoing, ("expert", "helper"), split_axis=0, concat_axis=0, tiled=True)


def routed_body(activations, expert_ids, route_gates, inner_weight, outer_weight):
    tok_count, model_width = activations.shape
    top_count = expert_ids.shape[1]
    devices_all = lax.axis_size("expert") * lax.axis_size("helper")
    experts_all = devices_all // 2
    capacity = 2 * max(1, tok_count * top_count // experts_all)
    half_cap = capacity // 2
    flat_ids = expert_ids.reshape(-1)
    onehot = (flat_ids[:, None] == jnp.arange(experts_all, dtype=jnp.int32)[None, :]).astype(
        jnp.int32
    )
    ranking = jnp.sum(jnp.cumsum(onehot, axis=0) * onehot, axis=1) - 1
    slot_index = flat_ids * capacity + ranking
    token_index = jnp.arange(flat_ids.shape[0], dtype=jnp.int32) // top_count
    buffer = jnp.zeros((experts_all * capacity, model_width), activations.dtype)
    buffer = buffer.at[slot_index].set(activations[token_index])
    parity = lax.axis_index("helper") % 2
    arrived = deliver(jnp.repeat(buffer.reshape(experts_all, capacity, model_width), 2, axis=0))
    slot_rows = arrived.reshape(-1, model_width)
    projected = jnp.einsum(
        "rd,cdf->crf", slot_rows, inner_weight[0], preferred_element_type=jnp.float32
    )
    gate_proj = projected[0]
    up_proj = projected[1]
    hidden = ((up_proj + 1.0) * gate_proj * jax.nn.sigmoid(1.702 * gate_proj)).astype(jnp.bfloat16)
    partial_value = jnp.dot(hidden, outer_weight[0], preferred_element_type=jnp.float32).astype(
        jnp.bfloat16
    )
    partial_value = partial_value.reshape(devices_all, capacity, model_width)
    first_part = partial_value[:, :half_cap]
    second_part = partial_value[:, half_cap:]
    kept_half = jnp.where(parity == 0, first_part, second_part)
    given_half = jnp.where(parity == 0, second_part, first_part)
    received_half = swapped(given_half, "helper", 0)
    kept_half = lax.optimization_barrier(kept_half)
    summed = kept_half.astype(jnp.float32) + received_half.astype(jnp.float32)
    results = summed.astype(jnp.bfloat16)
    returned = send_back(results).reshape(experts_all * capacity, model_width)
    picked = returned[slot_index].astype(jnp.float32).reshape(tok_count, top_count, model_width)
    combined = jnp.sum(picked * route_gates[:, :, None], axis=1)
    return combined.astype(jnp.bfloat16)


AXES = ("expert", "helper")


def dense_body(activations, expert_ids, route_gates, inner_weight, outer_weight):
    experts_all = lax.axis_size("expert") * lax.axis_size("helper") // 2
    expert = (lax.axis_index("expert") * lax.axis_size("helper") + lax.axis_index("helper")) // 2
    named = expert_ids[:, :, None] == jnp.arange(experts_all, dtype=jnp.int32)[None, None, :]
    weights = jnp.sum(jnp.where(named, route_gates[:, :, None], 0.0), axis=1)
    rows = lax.all_gather(activations, AXES, axis=0, tiled=True)
    weights = lax.all_gather(weights, AXES, axis=0, tiled=True)
    own = jnp.sum(jnp.where(jnp.arange(experts_all)[None, :] == expert, weights, 0.0), axis=1)
    gate_proj = jnp.dot(rows, inner_weight[0, 0], preferred_element_type=jnp.float32)
    up_proj = jnp.dot(rows, inner_weight[0, 1], preferred_element_type=jnp.float32)
    hidden = ((up_proj + 1.0) * gate_proj * jax.nn.sigmoid(1.702 * gate_proj)).astype(jnp.bfloat16)
    partial = jnp.dot(hidden, outer_weight[0], preferred_element_type=jnp.float32)
    partial = (partial * own[:, None]).astype(jnp.bfloat16)
    return lax.psum_scatter(partial, AXES, scatter_dimension=0, tiled=True)


UP, DOWN, ACROSS, TWIN = 0, 1, 2, 3


def line_kernel(
    rows_ref, inner_ref, outer_ref, out_ref,
    rows, inner, outer, parts, twin_in, cross_out, cross_in, line_out, line_up, line_down,
    gather_send, gather_recv, twin_send, twin_recv, cross_send, cross_recv, late_out, late_in, late_sem,
    up_send, up_recv, down_send, down_recv, weight_sem,
):
    length = 4
    tok, width = out_ref.shape
    me = lax.axis_index("expert")
    z = lax.axis_index("helper")
    x, core = me // 2, me % 2
    spare = rows_ref.shape[1] - 128
    experts_all = lax.axis_size("expert") * lax.axis_size("helper") // 2
    expert = (me * length + z) // 2
    up_dev = {"helper": jnp.minimum(z + 1, length - 1)}
    down_dev = {"helper": jnp.maximum(z - 1, 0)}
    cross_dev = {"expert": (1 - x) * 2 + core}
    twin_dev = {"expert": x * 2 + (1 - core)}
    devs = (up_dev, down_dev, cross_dev, twin_dev)
    has_up, has_down = z < length - 1, z > 0
    at_end = (z == 0) | (z == length - 1)
    half = tok - 16
    nearest = jnp.where(z <= 1, 2, 1)
    own_slot = core * 2 + x
    cross_slot = core * 2 + (1 - x)

    load_inner = pltpu.make_async_copy(inner_ref, inner, weight_sem.at[0])
    load_outer = pltpu.make_async_copy(outer_ref, outer, weight_sem.at[1])
    load_inner.start()
    load_outer.start()

    barrier = pltpu.get_barrier_semaphore()

    def greet(dev):
        pl.semaphore_signal(barrier, inc=1, device_id=dev, device_id_type=pl.DeviceIdType.MESH)

    greet(cross_dev)
    greet(twin_dev)

    @pl.when(has_up)
    def _():
        greet(up_dev)

    @pl.when(has_down)
    def _():
        greet(down_dev)

    rows[z, own_slot] = rows_ref[...]
    pl.semaphore_wait(barrier, jnp.where(has_up & has_down, 4, 3))

    def block_copy(way, plane, slot):
        return pltpu.make_async_remote_copy(
            src_ref=rows.at[plane, slot], dst_ref=rows.at[plane, slot],
            send_sem=gather_send.at[way, plane, slot], recv_sem=gather_recv.at[plane, slot],
            device_id=devs[way], device_id_type=pl.DeviceIdType.MESH,
        )

    def sem_at(ref, at):
        return ref.at[at[0], at[1]] if isinstance(at, tuple) else ref.at[at]

    def moved(src, dst, send, recv, dev, at):
        return pltpu.make_async_remote_copy(
            src_ref=src, dst_ref=sem_at(dst, at), send_sem=sem_at(send, at), recv_sem=sem_at(recv, at),
            device_id=dev, device_id_type=pl.DeviceIdType.MESH,
        )

    def twin_copy(plane):
        return moved(parts.at[plane, pl.ds((1 - core) * 2, 2)], twin_in, twin_send, twin_recv, twin_dev, plane)

    def cross_copy(plane):
        return moved(cross_out.at[plane], cross_in, cross_send, cross_recv, cross_dev, plane)

    def span(piece):
        return pl.ds(0, tok - half if piece else half)

    def line_copy(src, dst, send, recv, dev, plane, piece):
        return pltpu.make_async_remote_copy(
            src_ref=src.at[plane, piece, span(piece)], dst_ref=dst.at[plane, piece, span(piece)],
            send_sem=send.at[plane, piece], recv_sem=recv.at[plane, piece],
            device_id=dev, device_id_type=pl.DeviceIdType.MESH,
        )

    def up_copy(plane, piece):
        return line_copy(line_out, line_up, up_send, up_recv, up_dev, plane, piece)

    def down_copy(plane, piece):
        return line_copy(line_out, line_down, down_send, down_recv, down_dev, plane, piece)

    def late_copy():
        return pltpu.make_async_remote_copy(
            src_ref=late_out, dst_ref=late_in, send_sem=late_sem.at[0], recv_sem=late_sem.at[1],
            device_id=cross_dev, device_id_type=pl.DeviceIdType.MESH,
        )

    def plane_of(i):
        second = jnp.where(z == 0, 1, z - 1)
        third = jnp.where(z == 0, 2, jnp.where(z == 3, 1, z + 1))
        fourth = jnp.where(z <= 1, 3, 0)
        return jnp.where(i == 0, z, jnp.where(i == 1, second, jnp.where(i == 2, third, fourth)))

    @pl.when(has_up)
    def _():
        block_copy(UP, z, own_slot).start()

    @pl.when(has_down)
    def _():
        block_copy(DOWN, z, own_slot).start()

    block_copy(ACROSS, z, own_slot).start()
    block_copy(TWIN, z, own_slot).start()

    def shift_in(dist):
        @pl.when(z - dist >= 0)
        def _():
            plane = jnp.maximum(z - dist, 0)
            block_copy(UP, plane, own_slot).wait_recv()

            @pl.when(has_up)
            def _():
                block_copy(UP, plane, own_slot).start()

            block_copy(ACROSS, plane, own_slot).start()
            block_copy(TWIN, plane, own_slot).start()

        @pl.when(z + dist <= length - 1)
        def _():
            plane = jnp.minimum(z + dist, length - 1)
            block_copy(DOWN, plane, own_slot).wait_recv()

            @pl.when(has_down)
            def _():
                block_copy(DOWN, plane, own_slot).start()

            block_copy(ACROSS, plane, own_slot).start()
            block_copy(TWIN, plane, own_slot).start()

    def expert_part(plane):
        group = rows[plane].reshape(4 * tok, rows_ref.shape[1])
        lane = lax.broadcasted_iota(jnp.int32, (4 * tok, 128), 1)
        first = width - spare + expert
        mine = (lane == first) | (lane == first + experts_all) | (lane == first + 2 * experts_all)
        tail = rows[plane, :, :, pl.ds(spare, 128)].reshape(4 * tok, 128).astype(jnp.float32)
        gain = jnp.sum(jnp.where(mine, tail, 0.0), axis=1, keepdims=True)
        group = group[:, :width]
        over = (((1,), (1,)), ((), ()))
        gate_proj = lax.dot_general(group, inner[0], over, preferred_element_type=jnp.float32)
        up_proj = lax.dot_general(group, inner[1], over, preferred_element_type=jnp.float32)
        hidden = ((up_proj + 1.0) * gate_proj * jax.nn.sigmoid(1.702 * gate_proj)).astype(jnp.bfloat16)
        for low in range(0, width, 1024):
            high = min(low + 1024, width)
            value = jnp.dot(hidden, outer[:, low:high], preferred_element_type=jnp.float32) * gain
            parts[plane, :, :, low:high] = value.astype(jnp.bfloat16).reshape(4, tok, high - low)

    near, far = slice(0, half), slice(half, tok)

    def pair_sum(plane, slot, source, span):
        return parts[plane, slot, span].astype(jnp.float32) + twin_in[plane, source, span].astype(jnp.float32)

    def cross_sum(plane):
        twin_copy(plane).wait_recv()
        cross_out[plane] = pair_sum(plane, cross_slot, 1 - x, near).astype(jnp.bfloat16)
        cross_copy(plane).start()

    def piece_sum(plane, piece):
        if piece == 1:
            return pair_sum(plane, cross_slot, 1 - x, far)
        if piece == 2:
            return pair_sum(plane, own_slot, x, far)
        cross_copy(plane).wait_recv()
        return pair_sum(plane, own_slot, x, near) + cross_in[plane].astype(jnp.float32)

    def line_first(plane, piece):
        line_out[plane, piece, span(piece)] = piece_sum(plane, piece).astype(jnp.bfloat16)

        @pl.when(z == 0)
        def _():
            up_copy(plane, piece).start()

        @pl.when(z == length - 1)
        def _():
            down_copy(plane, piece).start()

    def line_next(plane, piece):
        total = piece_sum(plane, piece)

        @pl.when(plane > z)
        def _():
            up_copy(plane, piece).wait_recv()
            line_out[plane, piece, span(piece)] = (total + line_up[plane, piece, span(piece)].astype(jnp.float32)).astype(jnp.bfloat16)
            up_copy(plane, piece).start()

        @pl.when(plane < z)
        def _():
            down_copy(plane, piece).wait_recv()
            line_out[plane, piece, span(piece)] = (total + line_down[plane, piece, span(piece)].astype(jnp.float32)).astype(jnp.bfloat16)
            down_copy(plane, piece).start()

    def step(i, carry):
        plane = plane_of(i)

        @pl.when(i < length - 1)
        def _():
            shift_in(i + 1)

        block_copy(ACROSS, plane, cross_slot).wait_recv()
        block_copy(TWIN, plane, cross_slot).start()

        @pl.when(jnp.logical_not(at_end) & (i == length - 1))
        def _():
            line_next(nearest, 1)
            line_next(nearest, 2)

        for other in range(2):
            block_copy(TWIN, plane, (1 - core) * 2 + other).wait_recv()

        @pl.when(i == 0)
        def _():
            load_inner.wait()
            load_outer.wait()

        expert_part(plane)
        twin_copy(plane).start()

        @pl.when(i >= 1)
        def _():
            cross_sum(plane)

        @pl.when(at_end & (i >= 1))
        def _():
            line_first(plane, 1)
            line_first(plane, 2)

        @pl.when(at_end & (i >= 2))
        def _():
            line_first(plane_of(i - 1), 0)

        return carry

    lax.fori_loop(0, length, step, 0)
    cross_sum(z)

    @pl.when(at_end)
    def _():
        line_first(plane_of(length - 1), 0)

    def line_step(j, carry):
        plane = jnp.where((z <= 1) == (j == 0), 3, 0)
        for piece in (1, 2, 0):
            line_next(plane, piece)
        return carry

    @pl.when(jnp.logical_not(at_end))
    def _():
        line_next(nearest, 0)
        lax.fori_loop(0, 2, line_step, 0)

    def arrived(piece):
        @pl.when(has_down)
        def _():
            up_copy(z, piece).wait_recv()

        @pl.when(has_up)
        def _():
            down_copy(z, piece).wait_recv()

        from_below = jnp.where(has_down, line_up[z, piece, span(piece)].astype(jnp.float32), 0.0)
        from_above = jnp.where(has_up, line_down[z, piece, span(piece)].astype(jnp.float32), 0.0)
        return piece_sum(z, piece) + from_below + from_above

    @pl.when(z == 0)
    def _():
        line_up[z] = jnp.zeros(line_up.shape[1:], jnp.bfloat16)

    @pl.when(z == length - 1)
    def _():
        line_down[z] = jnp.zeros(line_down.shape[1:], jnp.bfloat16)

    late_out[...] = arrived(1).astype(jnp.bfloat16)
    late_copy().start()
    out_ref[near] = arrived(0).astype(jnp.bfloat16)
    own = arrived(2)
    late_copy().wait_recv()
    out_ref[far] = (own + late_in[...].astype(jnp.float32)).astype(jnp.bfloat16)
    late_copy().wait_send()

    def drain(plane, carry):
        @pl.when(has_up & (plane <= z))
        def _():
            block_copy(UP, plane, own_slot).wait_send()

        @pl.when(has_down & (plane >= z))
        def _():
            block_copy(DOWN, plane, own_slot).wait_send()

        block_copy(ACROSS, plane, own_slot).wait_send()
        block_copy(TWIN, plane, own_slot).wait_send()
        block_copy(TWIN, plane, cross_slot).wait_send()
        twin_copy(plane).wait_send()
        cross_copy(plane).wait_send()

        @pl.when(plane > z)
        def _():
            for piece in range(3):
                up_copy(plane, piece).wait_send()

        @pl.when(plane < z)
        def _():
            for piece in range(3):
                down_copy(plane, piece).wait_send()

        return carry

    lax.fori_loop(0, length, drain, 0)


def line_body(activations, expert_ids, route_gates, inner_weight, outer_weight):
    tok, width = activations.shape
    hidden = outer_weight.shape[1]
    length = lax.axis_size("helper")
    experts_all = lax.axis_size("expert") * length // 2
    named = expert_ids[:, :, None] == jnp.arange(experts_all, dtype=jnp.int32)[None, None, :]
    weights = jnp.sum(jnp.where(named, route_gates[:, :, None], 0.0), axis=1)
    high = lax.reduce_precision(weights, 8, 7)
    middle = lax.reduce_precision(weights - high, 8, 7)
    low = weights - high - middle
    gates = jnp.concatenate([high, middle, low], axis=1).astype(jnp.bfloat16)
    whole = -(-width // 128) * 128
    rows = jnp.concatenate([activations, jnp.pad(gates, ((0, 0), (0, whole - width - gates.shape[1])))], axis=1)
    inner = jnp.swapaxes(inner_weight[0], 1, 2)
    bf16 = jnp.bfloat16
    dma = pltpu.SemaphoreType.DMA
    half = tok - 16
    halves = pltpu.VMEM((length, half, width), bf16)
    line = pltpu.VMEM((length, 3, half, width), bf16)
    return pl.pallas_call(
        line_kernel,
        out_shape=jax.ShapeDtypeStruct((tok, width), bf16),
        in_specs=[
            pl.BlockSpec(memory_space=pltpu.VMEM),
            pl.BlockSpec(memory_space=pl.ANY),
            pl.BlockSpec(memory_space=pl.ANY),
        ],
        out_specs=pl.BlockSpec(memory_space=pltpu.VMEM),
        scratch_shapes=[
            pltpu.VMEM((length, 4, tok, whole), bf16),
            pltpu.VMEM((2, hidden, width), bf16),
            pltpu.VMEM((hidden, width), bf16),
            pltpu.VMEM((length, 4, tok, width), bf16),
            pltpu.VMEM((length, 2, tok, width), bf16),
            halves, halves, line, line, line,
            dma((4, length, 4)), dma((length, 4)),
            dma((length,)), dma((length,)), dma((length,)), dma((length,)),
            pltpu.VMEM((tok - half, width), bf16), pltpu.VMEM((tok - half, width), bf16), dma((2,)),
            dma((length, 3)), dma((length, 3)), dma((length, 3)), dma((length, 3)),
            dma((2,)),
        ],
        compiler_params=pltpu.CompilerParams(
            collective_id=0, has_side_effects=True, vmem_limit_bytes=58 * 1024 * 1024
        ),
    )(rows, inner, outer_weight[0])


def body(activations, expert_ids, route_gates, inner_weight, outer_weight):
    tok_count, top_count = expert_ids.shape
    experts_all = lax.axis_size("expert") * lax.axis_size("helper") // 2
    capacity = 2 * max(1, tok_count * top_count // experts_all)
    spare = -activations.shape[1] % 128
    four = lax.axis_size("expert") == 4 and lax.axis_size("helper") == 4
    if capacity < tok_count:
        chosen = routed_body
    elif four and tok_count % 32 == 0 and spare >= 3 * experts_all:
        chosen = line_body
    else:
        chosen = dense_body
    return chosen(activations, expert_ids, route_gates, inner_weight, outer_weight)


def solution(mesh):
    placed = (
        P(("groups", "expert", "helper"), None),
        P(("groups", "expert", "helper"), None),
        P(("groups", "expert", "helper"), None),
        P(("expert", "helper"), None, None, None),
        P(("expert", "helper"), None, None),
    )
    return jax.shard_map(
        body,
        mesh=mesh,
        in_specs=placed,
        out_specs=P(("groups", "expert", "helper"), None),
        check_vma=False,
    )
```
